32 devices in a mesh: tile: 16 (over z, y, core), head: 2 (over x).
Axes of the slice: x: 2, y: 2, z: 4, core: 2. Of those that a mesh axis runs over, the one named last changes fastest.
Arguments:
- query_rows: bfloat16 [6144, 5120], P('tile', 'head'), may hold values from -60 to 60
- key_rows: bfloat16 [6144, 5120], P('tile', 'head'), may hold values from -60 to 60
- value_rows: bfloat16 [6144, 5120], P('tile', 'head'), may hold values from -6 to 6
- gain_q: float32 [5120], P('head'), may hold values from 0.1 to 1.9
- gain_k: float32 [5120], P('head'), may hold values from 0.1 to 1.9
- mem_keys: bfloat16 [256, 8, 5120], P('tile', None, 'head'), may hold values from -6 to 6
- mem_values: bfloat16 [256, 8, 5120], P('tile', None, 'head'), may hold values from -6 to 6
- tile_len: int32 [16], P('tile'), may hold values from 1 to 384, 4608 in all
- session: int32 [16], P('tile'), may hold values from 0 to 5, never falling along the last dimension, each value on 1 to 5 neighbouring positions
- req_owner: int32 [1024, 1], P('tile'), may hold values from 0 to 15; in each aligned block of 64 rows (0 to 63, 64 to 127, ...) at most 8 rows name the same one
- requested_block_index: int32 [1024], P('tile'), may hold values from 0 to 15
Outputs:
- attended: bfloat16 [6144, 5120], P('tile', 'head')
The draws below stay inside these ranges and needn't reach their ends.
Inputs may be any that keep to these rules, and one draw needn't show every extreme that they name: Each session's tiles stand in a row, the session numbers never falling along tiles; a session has 1 to 5 tiles. `req_owner`: among the 64 requests of one tile at most 8 name the same owner, and exactly 8 do for some owner and tile.
All inputs are finite; a program needn't handle non-finite values. No bound on the sum of `tile_len` on one device may be relied on, other than what follows from the above.
Results may differ from the reference program's by a relative error of at most 0.011.
Values may be sent and summed in bfloat16 or wider, within the bound.
No kernel may reach another device: no remote copies, remote signals or barrier semaphores. Data moves between devices by JAX's collectives and lax.ppermute only.
A program may use at most 64 MiB of HBM per device.

```python
import math
import jax
import jax.numpy as jnp
import numpy as np
from jax import lax

HEADS = 40
HEAD_DIM = 128
WIDTH = 5120
TILE_CAP = 384
EDGE = 64
BLOCK = 8
RETR = 64
BLK_DEV = 16
SESSIONS = 6
N_TILE_SEG = 5
SLOT = 8
TOKENS = 6144
MEMB = 256
RTOT = 1024
N_TILE = 16


def shared_fields(key):
    keys_all = jax.random.split(jax.random.fold_in(key, 17), 5)
    base_query = jax.random.normal(keys_all[0], (TOKENS, WIDTH), jnp.float32)
    base_key = jax.random.normal(keys_all[1], (TOKENS, WIDTH), jnp.float32)
    column_pos = jnp.arange(WIDTH, dtype=jnp.float32) / WIDTH
    column_scale = 0.6 * 3.0 ** column_pos * jnp.exp(jax.random.uniform(keys_all[2], (WIDTH,), jnp.float32, -0.7, 0.7))
    row_query = 0.4 * jnp.exp(jax.random.uniform(keys_all[3], (TOKENS, 1), jnp.float32, 0.0, 2.3))
    row_key = 0.4 * jnp.exp(jax.random.uniform(keys_all[4], (TOKENS, 1), jnp.float32, 0.0, 2.3))
    query_field = jnp.clip(base_query * row_query * column_scale[None, :], -60.0, 60.0)
    key_field = jnp.clip(base_key * row_key * column_scale[None, :], -60.0, 60.0)
    return (query_field, key_field)


def draw_query_rows(key, part):
    query_field, key_field = shared_fields(key)
    return query_field.astype(jnp.bfloat16)


def draw_key_rows(key, part):
    query_field, key_field = shared_fields(key)
    return key_field.astype(jnp.bfloat16)


def plant(values, own_key, smallest, high):
    place = [jax.random.randint(jax.random.fold_in(own_key, axis), (), 0, length) for axis, length in enumerate(values.shape)]
    longest = values.shape.index(max(values.shape))
    neighbour = place[:longest] + [(place[longest] + 1) % values.shape[longest]] + place[longest + 1:]
    return values.at[tuple(place)].set(smallest).at[tuple(neighbour)].set(high)


def block_levels(key, extent, shards, low, top_value):
    def one(dim, parts):
        heights = jax.random.uniform(jax.random.fold_in(jax.random.fold_in(key, 6), dim), (parts,), jnp.float32, low / len(shards), top_value / len(shards))
        return jnp.repeat(jnp.exp(heights), extent[dim] // parts).reshape((-1,) + (1,) * (len(extent) - dim - 1))

    level = one(*shards[0])
    for cut in shards[1:]:
        level = level * one(*cut)
    return level


def split_up(amount, total, most, skew):
    loads = [(1 << 20) // math.isqrt(standing ** skew) + 1 for standing in range(2, amount + 1)]
    spare, holding = total - most - (amount - 1), [1] * (amount - 1)
    while spare > 0:
        candidates = [i for i in range(amount - 1) if holding[i] < most]
        whole, budget = sum([loads[i] for i in candidates]), spare
        for i in candidates:
            extra = min(most - holding[i], max(1, budget * loads[i] // whole), spare)
            holding[i] = holding[i] + extra
            spare = spare - extra
    return np.array([most] + holding)


def uneven(own_key, number_of, total, limit, skew):
    if number_of == 2:
        one = jax.random.randint(own_key, (), max(1, total - limit), min(limit, total - 1) + 1)
        return jnp.stack([one, total - one])
    lengths = jnp.asarray(split_up(number_of, total, limit, skew), jnp.int32)
    pairs = (number_of - 1) // 2
    giver, taker = lengths[1:1 + 2 * pairs:2], lengths[2:2 + 2 * pairs:2]
    room = jnp.minimum(giver - 1, limit - taker)
    passed = jax.random.randint(jax.random.fold_in(own_key, 1), (pairs,), 0, 1 << 20) % (room + 1)
    lengths = lengths.at[1:1 + 2 * pairs:2].set(giver - passed).at[2:2 + 2 * pairs:2].set(taker + passed)
    return lengths[jax.random.permutation(jax.random.fold_in(own_key, 2), number_of)]


def routed_block(stream_key, own, number, rows, count, top, limit, slope):
    sequence = jax.random.permutation(stream_key, count)
    crowded, usual = shares(count, rows * top, limit, slope, True), shares(count, rows * top, limit, slope, False)
    places = jnp.arange(count)

    def named(lengths, rotation):
        used = int((lengths > 0).sum())
        fixed = max(1, used // 4)
        passed = fixed + (places - fixed + rotation * (used - fixed)) % max(1, count - fixed)
        return jnp.zeros((count,), jnp.int32).at[sequence[jnp.where(places < fixed, places, passed)]].set(jnp.asarray(lengths, jnp.int32))

    lengths = jnp.where(number % 4 == 0, named(crowded, number // 4), named(usual, number - number // 4 - 1))
    mixed = jax.random.permutation(jax.random.fold_in(own, 3), count)
    source_of, taker = mixed[0:count // 2 * 2:2], mixed[1:count // 2 * 2:2]
    margin = jnp.minimum(lengths[source_of] - 1, limit - lengths[taker]) // 2
    margin = jnp.where((source_of == sequence[0]) | (taker == sequence[0]) | (lengths[taker] == 0), 0, jnp.maximum(margin, 0))
    passed = jax.random.randint(jax.random.fold_in(own, 4), (count // 2,), 0, 1 << 20) % (margin + 1)
    lengths = lengths.at[source_of].add(-passed).at[taker].add(passed)
    items = jnp.searchsorted(jnp.cumsum(lengths), jnp.arange(rows * top), side="right").astype(jnp.int32)
    grid = items.reshape(top, rows).T
    grid = grid[jax.random.permutation(jax.random.fold_in(own, 1), rows)]
    rotation = jax.random.randint(jax.random.fold_in(own, 2), (rows, 1), 0, top)
    return jnp.take_along_axis(grid, (jnp.arange(top)[None, :] + rotation) % top, axis=1)


def shares(count, total, most, skew, full):
    loads = [(1 << 20) // math.isqrt(standing ** skew) + 1 for standing in range(1, count + 1)]
    largest = most if full else min(most, max(-(-total // count), total * loads[0] // sum(loads)))
    least = 1 if total - largest >= count - 1 else 0
    given, surplus = [largest] + [least] * (count - 1), total - largest - least * (count - 1)
    while surplus > 0:
        free = [i for i in range(1, count) if given[i] < largest] or [i for i in range(1, count) if given[i] < most]
        mass, budget = sum([loads[i] for i in free]), surplus
        for i in free:
            more = min(most - given[i], max(1, budget * loads[i] // mass), surplus)
            given[i] = given[i] + more
            surplus = surplus - more
    return np.array(given)


def normal_values(rng, shape, deviation, most, shards=(), kind=jnp.bfloat16):
    values = jax.random.normal(rng, shape, jnp.float32) * deviation
    if len(shards) > 0:
        values = block_levels(rng, shape, shards, -0.22, 0.18) * values
    return jnp.clip(values, min=-most, max=most).astype(kind)


def setup_inputs(seed: int = 0) -> dict:
    keys = jax.random.split(jax.random.key(seed), 12)
    query_rows = draw_query_rows(jax.random.fold_in(keys[11], 71), 0)
    key_rows = draw_key_rows(jax.random.fold_in(keys[11], 71), 0)
    value_rows = normal_values(keys[2], (TOKENS, WIDTH), 1.0, 6.0, ((0, 16), (1, 2)))
    gain_q = jnp.clip(1.0 + 0.18 * jax.random.normal(keys[3], (WIDTH,), jnp.float32), 0.1, 1.9)
    gain_k = jnp.clip(1.0 + 0.18 * jax.random.normal(keys[4], (WIDTH,), jnp.float32), 0.1, 1.9)
    mem_keys = normal_values(keys[5], (MEMB, BLOCK, WIDTH), 1.0, 6.0, ((0, 16), (2, 2)))
    mem_values = normal_values(keys[6], (MEMB, BLOCK, WIDTH), 1.0, 6.0, ((0, 16), (2, 2)))
    tile_len = uneven(keys[7], N_TILE, N_TILE * TILE_CAP * 3 // 4, TILE_CAP, 2).astype(jnp.int32)
    session = jnp.searchsorted(jnp.cumsum(uneven(keys[8], SESSIONS, N_TILE, N_TILE_SEG, 1)), jnp.arange(N_TILE), side="right").astype(jnp.int32)
    req_owner_keys = jax.random.split(jax.random.fold_in(keys[9], 1), RTOT // RETR)
    req_owner_turns = jax.random.permutation(jax.random.fold_in(keys[9], 3), RTOT // RETR)
    req_owner = jax.vmap(lambda own, number: routed_block(jax.random.fold_in(keys[9], 2), own, number, RETR, N_TILE, 1, SLOT, 2))(req_owner_keys, req_owner_turns).reshape((RTOT, 1))
    requested_block_index = plant(jax.random.randint(keys[10], (RTOT,), 0, BLK_DEV), jax.random.fold_in(keys[10], 1), 0, BLK_DEV - 1).astype(jnp.int32)
    return {"query_rows": query_rows, "key_rows": key_rows, "value_rows": value_rows, "gain_q": gain_q, "gain_k": gain_k, "mem_keys": mem_keys, "mem_values": mem_values, "tile_len": tile_len, "session": session, "req_owner": req_owner, "requested_block_index": requested_block_index}


EPSILON = 1e-06

def norm_rows(raw_rows, gain):
    rows32 = raw_rows.astype(jnp.float32)
    mean_sq = lax.optimization_barrier(jnp.sum(rows32 * rows32, axis=-1, keepdims=True)) / WIDTH
    return (rows32 * lax.rsqrt(mean_sq + EPSILON) * gain.astype(jnp.float32)).astype(jnp.bfloat16)

def reference(query_rows, key_rows, value_rows, gain_q, gain_k, mem_keys, mem_values, tile_len, session, req_owner, requested_block_index):
    wanted = (req_owner[:, 0] * BLK_DEV + requested_block_index).astype(jnp.int32).reshape(N_TILE, RETR)
    edge_index = jnp.arange(EDGE, dtype=jnp.int32)
    slot_index = jnp.arange(TILE_CAP, dtype=jnp.int32)
    score_scale = 1.0 / HEAD_DIM ** 0.5

    def tile_rows(source, which):
        return lax.dynamic_slice_in_dim(source, (which * TILE_CAP).astype(jnp.int32), TILE_CAP, 0)

    def one_tile(which):
        before = jnp.maximum(which - 1, 0).astype(jnp.int32)
        after = jnp.minimum(which + 1, N_TILE - 1).astype(jnp.int32)
        query_norm = norm_rows(tile_rows(query_rows, which), gain_q)
        own_keys = norm_rows(tile_rows(key_rows, which), gain_k)
        own_values = tile_rows(value_rows, which)
        left_keys = norm_rows(tile_rows(key_rows, before), gain_k)
        left_values = tile_rows(value_rows, before)
        right_keys = norm_rows(tile_rows(key_rows, after), gain_k)
        right_values = tile_rows(value_rows, after)
        blank = jnp.zeros((EDGE, WIDTH), jnp.bfloat16)
        left_len = tile_len[before].astype(jnp.int32)
        tail_keys = lax.dynamic_slice_in_dim(jnp.concatenate([blank, left_keys], 0), left_len, EDGE, 0)
        tail_values = lax.dynamic_slice_in_dim(jnp.concatenate([blank, left_values], 0), left_len, EDGE, 0)
        left_ok = (which > 0) & (session[before] == session[which]) & (edge_index >= EDGE - left_len)
        right_ok = (which < N_TILE - 1) & (session[after] == session[which]) & (edge_index < tile_len[after])
        own_ok = slot_index < tile_len[which]
        memory_keys = jnp.take(mem_keys, wanted[which], axis=0).reshape(RETR * BLOCK, WIDTH)
        memory_values = jnp.take(mem_values, wanted[which], axis=0).reshape(RETR * BLOCK, WIDTH)
        all_keys = jnp.concatenate([own_keys, tail_keys, right_keys[:EDGE], memory_keys], 0)
        all_values = jnp.concatenate([own_values, tail_values, right_values[:EDGE], memory_values], 0)
        visible = jnp.concatenate([own_ok, left_ok, right_ok, jnp.ones((RETR * BLOCK,), bool)], 0)
        query32 = query_norm.astype(jnp.float32).reshape(TILE_CAP, HEADS, HEAD_DIM)
        key32 = all_keys.astype(jnp.float32).reshape(-1, HEADS, HEAD_DIM)
        value32 = all_values.astype(jnp.float32).reshape(-1, HEADS, HEAD_DIM)
        scores = jnp.einsum('qhd,khd->hqk', query32, key32) * score_scale
        scores = jnp.where(visible[None, None, :], scores, jnp.float32(-1e+30))
        top = lax.optimization_barrier(jnp.max(scores, axis=-1, keepdims=True))
        expo = jnp.exp(scores - top)
        weights = (expo / lax.optimization_barrier(jnp.sum(expo, axis=-1, keepdims=True))).astype(jnp.bfloat16)
        result = jnp.einsum('hqk,khd->qhd', weights.astype(jnp.float32), value32).reshape(TILE_CAP, WIDTH)
        return jnp.where(own_ok[:, None], result, jnp.float32(0.0)).astype(jnp.bfloat16)
    tiles_out = lax.map(one_tile, jnp.arange(N_TILE, dtype=jnp.int32))
    return tiles_out.reshape(TOKENS, WIDTH)
```

```python
import functools
import math

import jax
import jax.numpy as jnp
from jax import lax
from jax.experimental import pallas as pl
from jax.experimental.pallas import tpu as pltpu
from jax.sharding import PartitionSpec as P

HEAD_DIM = 128
WIDTH = 5120
EDGE = 64
EPSILON = 1e-06
HIDDEN = -1e30
VMEM_BYTES = 48 * 1024 * 1024


def passed_along(value, axis, steps):
    count = lax.axis_size(axis)
    first, last = (max(0, -steps), min(count, count - steps))
    return lax.ppermute(value, axis, [(source, source + steps) for source in range(first, last)])


def row_squares(raw_rows):
    rows32 = raw_rows.astype(jnp.float32)
    return jnp.sum(rows32 * rows32, axis=1)


def normalize(raw_rows, totals, gain):
    rows32 = raw_rows.astype(jnp.float32)
    factor = lax.rsqrt(totals / WIDTH + EPSILON)
    return (rows32 * factor[:, None] * gain).astype(jnp.bfloat16)


def chip_position(tile, levels):
    level, row = tile // 4, (tile // 2) % 2
    return level + row * (2 * levels - 1 - 2 * level)


def ring_pairs(count, step):
    levels = count // 4
    at = {(chip_position(t, levels), t % 2): t for t in range(count)}
    places = 2 * levels
    return [(at[p, c], at[(p + step) % places, c]) for p in range(places) for c in range(2)]


def across_t(first, second):
    return lax.dot_general(first, second, (((1,), (1,)), ((), ())), preferred_element_type=jnp.float32)


def across(first, second):
    return jnp.dot(first, second, preferred_element_type=jnp.float32)


def with_ones(values):
    return jnp.concatenate([values, jnp.ones(values.shape, values.dtype)], axis=1)


def near_kernel(heads_per_step, bias_ref, q_ref, k_ref, v_ref, ek_ref, ev_ref, acc_ref, top_ref, sum_ref):
    step = pl.program_id(0)
    lane = lax.broadcasted_iota(jnp.int32, top_ref.shape, 1)

    @pl.when(step == 0)
    def _():
        top_ref[...] = jnp.zeros_like(top_ref)
        sum_ref[...] = jnp.zeros_like(sum_ref)

    own = k_ref.shape[0]
    for j in range(heads_per_step):
        columns = slice(j * HEAD_DIM, (j + 1) * HEAD_DIM)
        query = q_ref[:, columns]
        near = across_t(query, k_ref[:, columns]) + bias_ref[:, :own]
        edge = across_t(query, ek_ref[:, columns]) + bias_ref[:, own:]
        top = jnp.maximum(jnp.max(near, axis=1, keepdims=True), jnp.max(edge, axis=1, keepdims=True))
        near = jnp.exp2(near - top).astype(jnp.bfloat16)
        edge = jnp.exp2(edge - top).astype(jnp.bfloat16)
        both = across(near, with_ones(v_ref[:, columns])) + across(edge, with_ones(ev_ref[:, columns]))
        acc_ref[:, columns] = both[:, :HEAD_DIM]
        here = lane == step * heads_per_step + j
        top_ref[...] = jnp.where(here, top, top_ref[...])
        sum_ref[...] = jnp.where(here, both[:, HEAD_DIM:], sum_ref[...])


def near_part(bias, query, keys, values, edge_keys, edge_values):
    rows, width = query.shape
    heads = width // HEAD_DIM
    per_step = 2 if heads % 2 == 0 else 1
    wide = per_step * HEAD_DIM
    keys_seen = keys.shape[0] + edge_keys.shape[0]

    def columns(array):
        return pl.BlockSpec((array.shape[0], wide), lambda i: (0, i))

    stat = jax.ShapeDtypeStruct((rows, 128), jnp.float32)
    stat_spec = pl.BlockSpec((rows, 128), lambda i: (0, 0))
    return pl.pallas_call(
        functools.partial(near_kernel, per_step),
        grid=(heads // per_step,),
        in_specs=[pl.BlockSpec(bias.shape, lambda i: (0, 0))]
        + [columns(array) for array in (query, keys, values, edge_keys, edge_values)],
        out_specs=[pl.BlockSpec((rows, wide), lambda i: (0, i)), stat_spec, stat_spec],
        out_shape=[jax.ShapeDtypeStruct((rows, width), jnp.float32), stat, stat],
        compiler_params=pltpu.CompilerParams(vmem_limit_bytes=VMEM_BYTES),
        cost_estimate=pl.CostEstimate(
            flops=4 * rows * keys_seen * width,
            bytes_accessed=10 * rows * width,
            transcendentals=rows * keys_seen * heads,
        ),
        name="near_part",
    )(bias, query, keys, values, edge_keys, edge_values)


def far_kernel(groups, heads_per_step, *refs):
    first_ref, block_ref, live_ref, q_ref, acc_ref, top_ref, sum_ref = refs[:7]
    key_pieces = refs[7 : 7 + groups]
    value_pieces = refs[7 + groups : 7 + 2 * groups]
    out_ref, keys, values, sems = refs[7 + 2 * groups :]
    step = pl.program_id(0)
    wanted = keys.shape[0]

    def copies(key_piece, value_piece, block, slot):
        return (
            pltpu.make_async_copy(key_piece.at[block], keys.at[slot], sems.at[0]),
            pltpu.make_async_copy(value_piece.at[block], values.at[slot], sems.at[1]),
        )

    @pl.when(step == 0)
    def _():
        for g in range(groups):

            def fetch(slot, carry, g=g):
                for copy in copies(key_pieces[g], value_pieces[g], block_ref[slot], slot):
                    copy.start()
                return carry

            lax.fori_loop(first_ref[g], first_ref[g + 1], fetch, 0)
        for array, sem in ((keys, sems.at[0]), (values, sems.at[1])):
            pltpu.make_async_copy(array, array, sem).wait()

    lane = lax.broadcasted_iota(jnp.int32, top_ref.shape, 1)
    for j in range(heads_per_step):
        columns = slice(j * HEAD_DIM, (j + 1) * HEAD_DIM)
        head = step * heads_per_step + j
        place = pl.ds(pl.multiple_of(head * HEAD_DIM, HEAD_DIM), HEAD_DIM)

        def flat(array):
            block = array[:, :, place].astype(jnp.float32)
            return block.reshape(wanted * array.shape[1], HEAD_DIM).astype(jnp.bfloat16)

        scores = across_t(q_ref[:, columns], flat(keys))
        here = lane == head
        top_near = jnp.sum(jnp.where(here, top_ref[...], 0.0), axis=1, keepdims=True)
        sum_near = jnp.sum(jnp.where(here, sum_ref[...], 0.0), axis=1, keepdims=True)
        top = jnp.maximum(top_near, jnp.max(scores, axis=1, keepdims=True))
        weights = jnp.exp2(scores - top).astype(jnp.bfloat16)
        kept = jnp.exp2(top_near - top)
        both = across(weights, with_ones(flat(values)))
        total = both[:, HEAD_DIM:] + kept * sum_near
        result = (both[:, :HEAD_DIM] + kept * acc_ref[:, columns]) / total
        out_ref[:, columns] = jnp.where(live_ref[...] > 0.0, result, 0.0).astype(out_ref.dtype)


def far_part(first, block, live, query, acc, top, total, key_pieces, value_pieces):
    rows, width = query.shape
    heads = width // HEAD_DIM
    per_step = 2 if heads % 2 == 0 else 1
    wide = per_step * HEAD_DIM
    groups, wanted = len(key_pieces), block.shape[0]
    tokens = key_pieces[0].shape[1]

    def columns(array):
        return pl.BlockSpec((array.shape[0], wide), lambda i: (0, i))

    def whole(array):
        return pl.BlockSpec(array.shape, lambda i: (0, 0))

    return pl.pallas_call(
        functools.partial(far_kernel, groups, per_step),
        grid=(heads // per_step,),
        in_specs=[pl.BlockSpec(memory_space=pltpu.SMEM)] * 2
        + [whole(live), columns(query), columns(acc), whole(top), whole(total)]
        + [pl.BlockSpec(memory_space=pl.ANY)] * (2 * groups),
        out_specs=pl.BlockSpec((rows, wide), lambda i: (0, i)),
        out_shape=jax.ShapeDtypeStruct((rows, width), jnp.bfloat16),
        scratch_shapes=[
            pltpu.VMEM((wanted, tokens, width), jnp.bfloat16),
            pltpu.VMEM((wanted, tokens, width), jnp.bfloat16),
            pltpu.SemaphoreType.DMA((2,)),
        ],
        compiler_params=pltpu.CompilerParams(vmem_limit_bytes=VMEM_BYTES),
        cost_estimate=pl.CostEstimate(
            flops=4 * rows * wanted * tokens * width,
            bytes_accessed=8 * rows * width + 4 * wanted * tokens * width,
            transcendentals=rows * wanted * tokens * heads,
        ),
        name="far_part",
    )(first, block, live, query, acc, top, total, *key_pieces, *value_pieces)


def per_device(
    query_rows,
    key_rows,
    value_rows,
    gain_q,
    gain_k,
    mem_keys,
    mem_values,
    tile_len,
    session,
    req_owner,
    requested_block_index,
):
    capacity, width_here = query_rows.shape
    count = lax.axis_size("tile")
    levels = count // 4
    places = 2 * levels
    me = lax.axis_index("tile")

    up, down = ring_pairs(count, 1), ring_pairs(count, -1)
    swap = [(t, t ^ 1) for t in range(count)]
    lane_keys, lane_values = [mem_keys], [mem_values]
    for _ in range(places - 1):
        lane_keys.append(lax.ppermute(lane_keys[-1], "tile", up))
        lane_values.append(lax.ppermute(lane_values[-1], "tile", down))
    other_keys = [lax.ppermute(piece, "tile", swap) for piece in lane_keys]
    other_values = [lax.ppermute(piece, "tile", swap) for piece in lane_values]
    key_pieces, value_pieces = [], []
    for d in range(places):
        key_pieces += [lane_keys[d], other_keys[d]]
        value_pieces += [lane_values[-d], other_values[-d]] if d else [lane_values[0], other_values[0]]

    owners = req_owner[:, 0]
    distance = (chip_position(me, levels) - chip_position(owners, levels)) % places
    group = distance * 2 + ((owners % 2) != (me % 2)).astype(jnp.int32)
    number = jnp.arange(group.shape[0], dtype=jnp.int32)
    rank_key = group * group.shape[0] + number
    rank = jnp.sum((rank_key[None, :] < rank_key[:, None]).astype(jnp.int32), axis=1)
    block = jnp.sum(jnp.where(rank[None, :] == number[:, None], requested_block_index[None, :], 0), axis=1)
    first = jnp.sum(
        (group[None, :] < jnp.arange(count + 1, dtype=jnp.int32)[:, None]).astype(jnp.int32), axis=1
    )

    my_length = tile_len[0]
    totals_q, totals_k = lax.psum((row_squares(query_rows), row_squares(key_rows)), "head")
    query_norm = normalize(query_rows, totals_q, gain_q * (math.log2(math.e) / HEAD_DIM**0.5))
    key_norm = normalize(key_rows, totals_k, gain_k)
    blank = jnp.zeros((EDGE, width_here), jnp.bfloat16)

    def tail(rows):
        return lax.dynamic_slice_in_dim(jnp.concatenate([blank, rows], 0), my_length, EDGE, 0)

    about = jnp.stack([session[0] + 1, my_length])
    left_keys, left_values, left = passed_along((tail(key_norm), tail(value_rows), about), "tile", 1)
    right_keys, right_values, right = passed_along(
        (key_norm[:EDGE], value_rows[:EDGE], about), "tile", -1
    )
    edge_index = jnp.arange(EDGE, dtype=jnp.int32)
    live_rows = jnp.arange(capacity, dtype=jnp.int32) < my_length
    visible = jnp.concatenate(
        [
            live_rows,
            (left[0] == about[0]) & (edge_index >= EDGE - left[1]),
            (right[0] == about[0]) & (edge_index < right[1]),
        ]
    )
    bias = jnp.where(visible, 0.0, jnp.float32(HIDDEN))[None, :]
    live = jnp.broadcast_to(live_rows[:, None], (capacity, HEAD_DIM)).astype(jnp.float32)
    edge_keys = jnp.concatenate([left_keys, right_keys], 0)
    edge_values = jnp.concatenate([left_values, right_values], 0)
    acc, top, total = near_part(bias, query_norm, key_norm, value_rows, edge_keys, edge_values)
    return far_part(first, block, live, query_norm, acc, top, total, key_pieces, value_pieces)


def solution(mesh):
    in_specs = (
        P("tile", "head"),
        P("tile", "head"),
        P("tile", "head"),
        P("head"),
        P("head"),
        P("tile", None, "head"),
        P("tile", None, "head"),
        P("tile"),
        P("tile"),
        P("tile", None),
        P("tile"),
    )
    out_specs = P("tile", "head")
    return jax.shard_map(
        per_device, mesh=mesh, in_specs=in_specs, out_specs=out_specs, check_vma=False
    )
```

```python
import functools
import math

import jax
import jax.numpy as jnp
from jax import lax
from jax.experimental import pallas as pl
from jax.experimental.pallas import tpu as pltpu
from jax.sharding import PartitionSpec as P

HEAD_DIM = 128
WIDTH = 5120
EDGE = 64
EPSILON = 1e-06
HIDDEN = -1e30
VMEM_BYTES = 48 * 1024 * 1024


def passed_along(value, axis, steps):
    count = lax.axis_size(axis)
    first, last = (max(0, -steps), min(count, count - steps))
    return lax.ppermute(value, axis, [(source, source + steps) for source in range(first, last)])


def row_squares(raw_rows):
    rows32 = raw_rows.astype(jnp.float32)
    return jnp.sum(rows32 * rows32, axis=1)


def normalize(raw_rows, totals, gain):
    rows32 = raw_rows.astype(jnp.float32)
    factor = lax.rsqrt(totals / WIDTH + EPSILON)
    return (rows32 * factor[:, None] * gain).astype(jnp.bfloat16)


def chip_position(tile, levels):
    level, row = tile // 4, (tile // 2) % 2
    return level + row * (2 * levels - 1 - 2 * level)


def ring_pairs(count, step):
    levels = count // 4
    at = {(chip_position(t, levels), t % 2): t for t in range(count)}
    places = 2 * levels
    return [(at[p, c], at[(p + step) % places, c]) for p in range(places) for c in range(2)]


def across_t(first, second):
    return lax.dot_general(first, second, (((1,), (1,)), ((), ())), preferred_element_type=jnp.float32)


def down_rows(first, second):
    return lax.dot_general(first, second, (((0,), (0,)), ((), ())), preferred_element_type=jnp.float32)


def attend(query, parts, before):
    scores = []
    for keys, _, bias in parts:
        wide = jnp.concatenate([bias] * (query.shape[0] // bias.shape[1]), axis=1)
        scores.append(across_t(keys, query) + wide)
    top = functools.reduce(jnp.maximum, [jnp.max(part, axis=0, keepdims=True) for part in scores])
    if before is not None:
        top = jnp.maximum(top, before[0])
    total, acc = jnp.float32(0.0), jnp.float32(0.0)
    for part, (_, values, _) in zip(scores, parts):
        weights = jnp.exp2(part - top)
        total = total + jnp.sum(weights, axis=0, keepdims=True)
        acc = acc + down_rows(values, weights.astype(jnp.bfloat16))
    if before is not None:
        kept = jnp.exp2(before[0] - top)
        total = total + kept * before[1]
        acc = acc + kept * before[2]
    return top, total, acc


def store_sums(sums, j, columns, top_ref, sum_ref, acc_ref):
    top, total, acc = sums
    top_ref[j] = jnp.broadcast_to(top, top_ref.shape[1:])
    sum_ref[j] = jnp.broadcast_to(total, sum_ref.shape[1:])
    acc_ref[columns, :] = acc


def near_kernel(per_step, bias_ref, q_ref, k_ref, v_ref, ek_ref, ev_ref, top_ref, sum_ref, acc_ref):
    own = k_ref.shape[0]
    for j in range(per_step):
        columns = slice(j * HEAD_DIM, (j + 1) * HEAD_DIM)
        parts = [
            (k_ref[:, columns], v_ref[:, columns], bias_ref[:own, :]),
            (ek_ref[:, columns], ev_ref[:, columns], bias_ref[own:, :]),
        ]
        sums = attend(q_ref[:, columns], parts, None)
        store_sums(sums, j, columns, top_ref, sum_ref, acc_ref)


def specs(width, rows):
    heads = width // HEAD_DIM
    per_step = 2 if heads % 2 == 0 else 1
    wide = per_step * HEAD_DIM
    stat = jax.ShapeDtypeStruct((heads, 8, rows), jnp.float32)
    stat_spec = pl.BlockSpec((per_step, 8, rows), lambda i: (i, 0, 0))
    acc = jax.ShapeDtypeStruct((width, rows), jnp.float32)
    acc_spec = pl.BlockSpec((wide, rows), lambda i: (i, 0))
    return heads, per_step, [stat, stat, acc], [stat_spec, stat_spec, acc_spec]


def columns_of(array, per_step):
    return pl.BlockSpec((array.shape[0], per_step * HEAD_DIM), lambda i: (0, i))


def whole(array):
    return pl.BlockSpec(array.shape, lambda i: (0, 0))


def cost(rows, seen, width):
    return pl.CostEstimate(
        flops=4 * rows * seen * width,
        bytes_accessed=10 * rows * width,
        transcendentals=rows * seen * width // HEAD_DIM,
    )


def near_part(bias, query, keys, values, edge_keys, edge_values):
    rows, width = query.shape
    heads, per_step, shapes, out_specs = specs(width, rows)
    arrays = (query, keys, values, edge_keys, edge_values)
    return pl.pallas_call(
        functools.partial(near_kernel, per_step),
        grid=(heads // per_step,),
        in_specs=[whole(bias)] + [columns_of(array, per_step) for array in arrays],
        out_specs=out_specs,
        out_shape=shapes,
        compiler_params=pltpu.CompilerParams(vmem_limit_bytes=VMEM_BYTES),
        cost_estimate=cost(rows, bias.shape[0], width),
        name="near_part",
    )(bias, *arrays)


def far_kernel(groups, per_step, last, *refs):
    first_ref, block_ref, bias_ref, q_ref, before_top, before_sum, before_acc = refs[:7]
    refs = refs[7:]
    if last:
        live_ref, refs = refs[0], refs[1:]
    *out_refs, keys, values, sems = refs[len(refs) - (4 if last else 6) :]
    pieces = refs[: len(refs) - len(out_refs) - 3]
    joined = len(pieces) == groups
    key_pieces, value_pieces = pieces[:groups], pieces if joined else pieces[groups:]
    offset = pieces[0].shape[0] // 2 if joined else 0
    step = pl.program_id(0)
    slots, tokens = keys.shape[:2]

    @pl.when(step == 0)
    def _():
        start = first_ref[0]

        def fetch_from(g):
            def fetch(slot, carry):
                block = block_ref[slot]
                to = slot - start
                pltpu.make_async_copy(key_pieces[g].at[block], keys.at[to], sems.at[0]).start()
                pltpu.make_async_copy(value_pieces[g].at[block + offset], values.at[to], sems.at[1]).start()
                return carry

            return fetch

        for g in range(groups):
            lax.fori_loop(first_ref[g], first_ref[g + 1], fetch_from(g), 0)
        lax.fori_loop(first_ref[groups], start + slots, fetch_from(0), 0)
        pltpu.make_async_copy(keys, keys, sems.at[0]).wait()
        pltpu.make_async_copy(values, values, sems.at[1]).wait()

    for j in range(per_step):
        columns = slice(j * HEAD_DIM, (j + 1) * HEAD_DIM)
        place = pl.ds(pl.multiple_of((step * per_step + j) * HEAD_DIM, HEAD_DIM), HEAD_DIM)

        def flat(array):
            block = array[:, :, place].astype(jnp.float32)
            return block.reshape(slots * tokens, HEAD_DIM).astype(jnp.bfloat16)

        before = (before_top[j, :1, :], before_sum[j, :1, :], before_acc[columns, :])
        sums = attend(q_ref[:, columns], [(flat(keys), flat(values), bias_ref[...])], before)
        if last:
            result = jnp.where(live_ref[...] > 0.0, sums[2] / sums[1], 0.0)
            out_refs[0][:, columns] = result.T.astype(out_refs[0].dtype)
        else:
            store_sums(sums, j, columns, *out_refs)


def far_part(name, first, block, slots, query, before, pieces, live=None):
    rows, width = query.shape
    heads, per_step, shapes, out_specs = specs(width, rows)
    in_specs = list(out_specs)
    groups, tokens = first.shape[0] - 1, pieces[0].shape[1]
    seen = slots * tokens
    token = jnp.arange(seen, dtype=jnp.int32)[:, None]
    bias = jnp.where(token < (first[-1] - first[0]) * tokens, 0.0, jnp.float32(HIDDEN))
    bias = jnp.broadcast_to(bias, (seen, 128))
    block = jnp.concatenate([block, jnp.zeros((slots,), jnp.int32)])
    if live is not None:
        shapes, out_specs = jax.ShapeDtypeStruct((rows, width), jnp.bfloat16), columns_of(query, per_step)
    extra = [] if live is None else [live]
    return pl.pallas_call(
        functools.partial(far_kernel, groups, per_step, live is not None),
        grid=(heads // per_step,),
        in_specs=[pl.BlockSpec(memory_space=pltpu.SMEM)] * 2
        + [whole(bias), columns_of(query, per_step)]
        + in_specs
        + [whole(array) for array in extra]
        + [pl.BlockSpec(memory_space=pl.ANY)] * len(pieces),
        out_specs=out_specs,
        out_shape=shapes,
        scratch_shapes=[
            pltpu.VMEM((slots, tokens, width), jnp.bfloat16),
            pltpu.VMEM((slots, tokens, width), jnp.bfloat16),
            pltpu.SemaphoreType.DMA((2,)),
        ],
        compiler_params=pltpu.CompilerParams(vmem_limit_bytes=VMEM_BYTES),
        cost_estimate=cost(rows, seen, width),
        name=name,
    )(first, block, bias, query, *before, *extra, *pieces)


def per_device(
    query_rows,
    key_rows,
    value_rows,
    gain_q,
    gain_k,
    mem_keys,
    mem_values,
    tile_len,
    session,
    req_owner,
    requested_block_index,
):
    capacity, width_here = query_rows.shape
    count = lax.axis_size("tile")
    levels = count // 4
    places = 2 * levels
    half = places // 2
    me = lax.axis_index("tile")

    owners = req_owner[:, 0]
    ahead = (chip_position(owners, levels) - chip_position(me, levels)) % places
    distance = jnp.minimum(ahead, places - ahead)
    side = 2 * (ahead > half).astype(jnp.int32)
    other = ((owners % 2) != (me % 2)).astype(jnp.int32)
    group = jnp.where(distance == 0, other, 4 * distance - 2 + side + other)
    number = jnp.arange(group.shape[0], dtype=jnp.int32)
    rank_key = group * group.shape[0] + number
    rank = jnp.sum((rank_key[None, :] < rank_key[:, None]).astype(jnp.int32), axis=1)
    block = jnp.sum(jnp.where(rank[None, :] == number[:, None], requested_block_index[None, :], 0), axis=1)
    first = jnp.sum(
        (group[None, :] < jnp.arange(count + 1, dtype=jnp.int32)[:, None]).astype(jnp.int32), axis=1
    )

    my_length = tile_len[0]
    blank = jnp.zeros((EDGE, width_here), jnp.bfloat16)

    def tail(rows):
        return lax.dynamic_slice_in_dim(jnp.concatenate([blank, rows], 0), my_length, EDGE, 0)

    about = jnp.stack([session[0] + 1, my_length])
    tails = jnp.concatenate([tail(key_rows), tail(value_rows)], 0)
    fronts = jnp.concatenate([key_rows[:EDGE], value_rows[:EDGE]], 0)
    from_left, left = passed_along((tails, about), "tile", 1)
    from_right, right = passed_along((fronts, about), "tile", -1)
    edge_keys = jnp.concatenate([from_left[:EDGE], from_right[:EDGE]], 0)
    edge_values = jnp.concatenate([from_left[EDGE:], from_right[EDGE:]], 0)
    totals_q, totals_k, totals_e = lax.psum(
        (row_squares(query_rows), row_squares(key_rows), row_squares(edge_keys)), "head"
    )
    query_norm = normalize(query_rows, totals_q, gain_q * (math.log2(math.e) / HEAD_DIM**0.5))
    key_norm = normalize(key_rows, totals_k, gain_k)
    edge_norm = normalize(edge_keys, totals_e, gain_k)
    edge_index = jnp.arange(EDGE, dtype=jnp.int32)
    live_rows = jnp.arange(capacity, dtype=jnp.int32) < my_length
    visible = jnp.concatenate(
        [
            live_rows,
            (left[0] == about[0]) & (edge_index >= EDGE - left[1]),
            (right[0] == about[0]) & (edge_index < right[1]),
        ]
    )
    bias = jnp.where(visible, 0.0, jnp.float32(HIDDEN))
    bias = jnp.broadcast_to(bias[:, None], (bias.shape[0], 128))
    live = live_rows[None, :].astype(jnp.float32)
    sums = near_part(bias, query_norm, key_norm, value_rows, edge_norm, edge_values)

    up, down = ring_pairs(count, 1), ring_pairs(count, -1)
    swap = [(t, t ^ 1) for t in range(count)]

    def moved(piece, pairs):
        return lax.ppermute(piece, "tile", pairs)

    def after(pieces, results):
        *pieces, top = lax.optimization_barrier((*pieces, results[0]))
        return pieces, [top, *results[1:]]

    own = jnp.concatenate([mem_keys, mem_values], 0)
    blocks = mem_keys.shape[0]
    below, above = own, own
    pieces = [own, moved(own, swap)]
    for step in range(1, half):
        below, above = moved(below, up), moved(above, down)
        if step == half - 2:
            (below, above), sums = after([below, above], sums)
        if step == half - 1:
            sums = far_part("far_part", first[: 4 * half - 5], block, number.shape[0], query_norm, sums, pieces)
            (below, above), sums = after([below, above], sums)
            pieces = []
        pieces += [above, moved(above, swap), below, moved(below, swap)]
    keys, values = moved(below[:blocks], up), moved(above[blocks:], down)
    most = 2 * number.shape[0] // count
    sums = far_part("far_next", first[4 * half - 6 : 4 * half - 1], block, 4 * most, query_norm, sums, pieces)
    (keys, values), sums = after([keys, values], sums)
    pieces = [keys, moved(keys, swap), values, moved(values, swap)]
    return far_part("far_last", first[4 * half - 2 :], block, 2 * most, query_norm, sums, pieces, live)


def solution(mesh):
    in_specs = (
        P("tile", "head"),
        P("tile", "head"),
        P("tile", "head"),
        P("head"),
        P("head"),
        P("tile", None, "head"),
        P("tile", None, "head"),
        P("tile"),
        P("tile"),
        P("tile", None),
        P("tile"),
    )
    out_specs = P("tile", "head")
    return jax.shard_map(
        per_device, mesh=mesh, in_specs=in_specs, out_specs=out_specs, check_vma=False
    )
```

```python
import functools
import math

import jax
import jax.numpy as jnp
from jax import lax
from jax.experimental import pallas as pl
from jax.experimental.pallas import tpu as pltpu
from jax.sharding import PartitionSpec as P

HEAD_DIM = 128
WIDTH = 5120
EDGE = 64
EPSILON = 1e-06
HIDDEN = -1e30
VMEM_BYTES = 32 * 1024 * 1024


def passed_along(value, axis, steps):
    count = lax.axis_size(axis)
    first, last = (max(0, -steps), min(count, count - steps))
    return lax.ppermute(value, axis, [(source, source + steps) for source in range(first, last)])


def row_squares(raw_rows):
    rows32 = raw_rows.astype(jnp.float32)
    return jnp.sum(rows32 * rows32, axis=1)


def normalize(raw_rows, totals, gain):
    rows32 = raw_rows.astype(jnp.float32)
    factor = lax.rsqrt(totals / WIDTH + EPSILON)
    return (rows32 * factor[:, None] * gain).astype(jnp.bfloat16)


def chip_position(tile, levels):
    level, row = tile // 4, (tile // 2) % 2
    return level + row * (2 * levels - 1 - 2 * level)


def ring_pairs(count, step):
    levels = count // 4
    at = {(chip_position(t, levels), t % 2): t for t in range(count)}
    places = 2 * levels
    return [(at[p, c], at[(p + step) % places, c]) for p in range(places) for c in range(2)]


def across_t(first, second):
    return lax.dot_general(first, second, (((1,), (1,)), ((), ())), preferred_element_type=jnp.float32)


def down_rows(first, second):
    return lax.dot_general(first, second, (((0,), (0,)), ((), ())), preferred_element_type=jnp.float32)


def attend(heads):
    scores = []
    for query, parts, _ in heads:
        wide = [jnp.concatenate([bias] * (query.shape[0] // bias.shape[1]), axis=1) for _, _, bias in parts]
        scores.append([across_t(keys, query) + add for (keys, _, _), add in zip(parts, wide)])
    tops = []
    for group, (_, _, before) in zip(scores, heads):
        found = [jnp.max(part, axis=0, keepdims=True) for part in group]
        tops.append(functools.reduce(jnp.maximum, found if before is None else found + [before[0]]))
    weights = [[jnp.exp2(part - top) for part in group] for group, top in zip(scores, tops)]
    results = []
    for group, top, (_, parts, before) in zip(weights, tops, heads):
        total = sum(jnp.sum(part, axis=0, keepdims=True) for part in group)
        acc = sum(down_rows(values, part.astype(jnp.bfloat16)) for part, (_, values, _) in zip(group, parts))
        if before is not None:
            kept = jnp.exp2(before[0] - top)
            total = total + kept * before[1]
            acc = acc + kept * before[2]
        results.append((top, total, acc))
    return results


def store_sums(sums, head, place, top_ref, sum_ref, acc_ref):
    top, total, acc = sums
    top_ref[head] = jnp.broadcast_to(top, top_ref.shape[1:])
    sum_ref[head] = jnp.broadcast_to(total, sum_ref.shape[1:])
    acc_ref[place, :] = acc


def over_heads(width, body):
    heads = width // HEAD_DIM
    together = max(n for n in (1, 2, 4, 5) if heads % n == 0 and (n < 5 or heads < 10))

    def some(i, carry):
        numbers = [i * together + j for j in range(together)]
        body([(head, pl.ds(pl.multiple_of(head * HEAD_DIM, HEAD_DIM), HEAD_DIM)) for head in numbers])
        return carry

    lax.fori_loop(0, heads // together, some, 0)


def near_kernel(bias_ref, q_ref, k_ref, v_ref, ek_ref, ev_ref, top_ref, sum_ref, acc_ref):
    own = k_ref.shape[0]

    def body(places):
        heads = []
        for _, place in places:
            parts = [
                (k_ref[:, place], v_ref[:, place], bias_ref[:own, :]),
                (ek_ref[:, place], ev_ref[:, place], bias_ref[own:, :]),
            ]
            heads.append((q_ref[:, place], parts, None))
        for (head, place), sums in zip(places, attend(heads)):
            store_sums(sums, head, place, top_ref, sum_ref, acc_ref)

    over_heads(q_ref.shape[1], body)


def sum_shapes(rows, width):
    stat = jax.ShapeDtypeStruct((width // HEAD_DIM, 8, rows), jnp.float32)
    return [stat, stat, jax.ShapeDtypeStruct((width, rows), jnp.float32)]


IN_VMEM = pl.BlockSpec(memory_space=pltpu.VMEM)


def cost(rows, seen, width):
    return pl.CostEstimate(
        flops=4 * rows * seen * width,
        bytes_accessed=10 * rows * width,
        transcendentals=rows * seen * width // HEAD_DIM,
    )


def near_part(bias, query, keys, values, edge_keys, edge_values):
    rows, width = query.shape
    return pl.pallas_call(
        near_kernel,
        in_specs=[IN_VMEM] * 6,
        out_specs=[IN_VMEM] * 3,
        out_shape=sum_shapes(rows, width),
        compiler_params=pltpu.CompilerParams(vmem_limit_bytes=VMEM_BYTES),
        cost_estimate=cost(rows, bias.shape[0], width),
        name="near_part",
    )(bias, query, keys, values, edge_keys, edge_values)


def far_kernel(groups, last, *refs):
    first_ref, block_ref, bias_ref, q_ref, before_top, before_sum, before_acc = refs[:7]
    refs = refs[7:]
    if last:
        live_ref, refs = refs[0], refs[1:]
    *out_refs, keys, values, sems = refs[len(refs) - (4 if last else 6) :]
    pieces = refs[: len(refs) - len(out_refs) - 3]
    joined = len(pieces) == groups
    key_pieces, value_pieces = pieces[:groups], pieces if joined else pieces[groups:]
    offset = pieces[0].shape[0] // 2 if joined else 0
    slots, tokens = keys.shape[:2]
    start = first_ref[0]

    def fetch_from(g):
        def fetch(slot, carry):
            block = block_ref[slot]
            to = slot - start
            pltpu.make_async_copy(key_pieces[g].at[block], keys.at[to], sems.at[0]).start()
            pltpu.make_async_copy(value_pieces[g].at[block + offset], values.at[to], sems.at[1]).start()
            return carry

        return fetch

    for g in range(groups):
        lax.fori_loop(first_ref[g], first_ref[g + 1], fetch_from(g), 0)
    lax.fori_loop(first_ref[groups], start + slots, fetch_from(0), 0)
    pltpu.make_async_copy(keys, keys, sems.at[0]).wait()
    pltpu.make_async_copy(values, values, sems.at[1]).wait()

    def flat(array, place):
        block = array[:, :, place].astype(jnp.float32)
        return block.reshape(slots * tokens, HEAD_DIM).astype(jnp.bfloat16)

    def body(places):
        heads = []
        for head, place in places:
            before = (before_top[head][:1, :], before_sum[head][:1, :], before_acc[place, :])
            heads.append((q_ref[:, place], [(flat(keys, place), flat(values, place), bias_ref[...])], before))
        for (head, place), sums in zip(places, attend(heads)):
            if last:
                result = jnp.where(live_ref[...] > 0.0, sums[2] / sums[1], 0.0)
                out_refs[0][:, place] = result.T.astype(out_refs[0].dtype)
            else:
                store_sums(sums, head, place, *out_refs)

    over_heads(q_ref.shape[1], body)


def far_part(name, first, block, slots, query, before, pieces, live=None):
    rows, width = query.shape
    groups, tokens = first.shape[0] - 1, pieces[0].shape[1]
    seen = slots * tokens
    token = jnp.arange(seen, dtype=jnp.int32)[:, None]
    bias = jnp.where(token < (first[-1] - first[0]) * tokens, 0.0, jnp.float32(HIDDEN))
    bias = jnp.broadcast_to(bias, (seen, 128))
    block = jnp.concatenate([block, jnp.zeros((slots,), jnp.int32)])
    extra = [] if live is None else [live]
    final = jax.ShapeDtypeStruct((rows, width), jnp.bfloat16)
    return pl.pallas_call(
        functools.partial(far_kernel, groups, live is not None),
        in_specs=[pl.BlockSpec(memory_space=pltpu.SMEM)] * 2
        + [IN_VMEM] * (5 + len(extra))
        + [pl.BlockSpec(memory_space=pl.ANY)] * len(pieces),
        out_specs=[IN_VMEM] * 3 if live is None else IN_VMEM,
        out_shape=sum_shapes(rows, width) if live is None else final,
        input_output_aliases={4: 0, 5: 1, 6: 2} if live is None else {},
        scratch_shapes=[
            pltpu.VMEM((slots, tokens, width), jnp.bfloat16),
            pltpu.VMEM((slots, tokens, width), jnp.bfloat16),
            pltpu.SemaphoreType.DMA((2,)),
        ],
        compiler_params=pltpu.CompilerParams(vmem_limit_bytes=VMEM_BYTES),
        cost_estimate=cost(rows, seen, width),
        name=name,
    )(first, block, bias, query, *before, *extra, *pieces)


def per_device(
    query_rows,
    key_rows,
    value_rows,
    gain_q,
    gain_k,
    mem_keys,
    mem_values,
    tile_len,
    session,
    req_owner,
    requested_block_index,
):
    capacity, width_here = query_rows.shape
    count = lax.axis_size("tile")
    levels = count // 4
    places = 2 * levels
    half = places // 2
    me = lax.axis_index("tile")

    owners = req_owner[:, 0]
    ahead = (chip_position(owners, levels) - chip_position(me, levels)) % places
    distance = jnp.minimum(ahead, places - ahead)
    side = 2 * (ahead > half).astype(jnp.int32)
    other = ((owners % 2) != (me % 2)).astype(jnp.int32)
    group = jnp.where(distance == 0, other, 4 * distance - 2 + side + other)
    number = jnp.arange(group.shape[0], dtype=jnp.int32)
    rank_key = group * group.shape[0] + number
    rank = jnp.sum((rank_key[None, :] < rank_key[:, None]).astype(jnp.int32), axis=1)
    block = jnp.sum(jnp.where(rank[None, :] == number[:, None], requested_block_index[None, :], 0), axis=1)
    first = jnp.sum(
        (group[None, :] < jnp.arange(count + 1, dtype=jnp.int32)[:, None]).astype(jnp.int32), axis=1
    )

    my_length = tile_len[0]
    totals_q, totals_k = lax.psum((row_squares(query_rows), row_squares(key_rows)), "head")
    query_norm = normalize(query_rows, totals_q, gain_q * (math.log2(math.e) / HEAD_DIM**0.5))
    key_norm = normalize(key_rows, totals_k, gain_k)
    live_rows = jnp.arange(capacity, dtype=jnp.int32) < my_length
    live = live_rows[None, :].astype(jnp.float32)
    own_label = (session[0] + 1).astype(jnp.bfloat16)
    edge_index = jnp.arange(EDGE, dtype=jnp.int32)
    blank = jnp.zeros((EDGE, width_here), jnp.bfloat16)

    def tail(rows):
        return lax.dynamic_slice_in_dim(jnp.concatenate([blank, rows], 0), my_length, EDGE, 0)

    def edge(keys, values, is_live):
        labels = jnp.where(is_live, own_label, jnp.bfloat16(0))
        return jnp.concatenate([keys, values, jnp.pad(labels[None, :], ((0, 15), (0, width_here - EDGE)))], 0)

    tails = edge(tail(key_norm), tail(value_rows), edge_index >= EDGE - my_length)
    fronts = edge(key_norm[:EDGE], value_rows[:EDGE], edge_index < my_length)
    from_left, from_right = passed_along(tails, "tile", 1), passed_along(fronts, "tile", -1)

    def near_sums(from_left, from_right):
        edge_keys = jnp.concatenate([from_left[:EDGE], from_right[:EDGE]], 0)
        edge_values = jnp.concatenate([from_left[EDGE : 2 * EDGE], from_right[EDGE : 2 * EDGE]], 0)
        labels = jnp.concatenate([from_left[2 * EDGE, :EDGE], from_right[2 * EDGE, :EDGE]])
        bias = jnp.where(jnp.concatenate([live_rows, labels == own_label]), 0.0, jnp.float32(HIDDEN))
        bias = jnp.broadcast_to(bias[:, None], (bias.shape[0], 128))
        return near_part(bias, query_norm, key_norm, value_rows, edge_keys, edge_values)

    up, down = ring_pairs(count, 1), ring_pairs(count, -1)
    swap = [(t, t ^ 1) for t in range(count)]

    def moved(piece, pairs):
        return lax.ppermute(piece, "tile", pairs)

    def after(pieces, results):
        *pieces, top = lax.optimization_barrier((*pieces, results[0]))
        return pieces, [top, *results[1:]]

    own = jnp.concatenate([mem_keys, mem_values], 0)
    blocks = mem_keys.shape[0]
    below, above = own, own
    pieces, unswapped = [], [own]
    for step in range(1, half):
        below, above = moved(below, up), moved(above, down)
        if step == 1:
            late, _, _ = lax.optimization_barrier((own, below, above))
            pieces, unswapped = [own, moved(late, swap)], []
            from_left, from_right, pieces[1] = lax.optimization_barrier((from_left, from_right, pieces[1]))
            sums = near_sums(from_left, from_right)
        unswapped += [above, below]
        if step == half - 2:
            unswapped, sums = after(unswapped, sums)
            below, above = unswapped[-1], unswapped[-2]
            for piece in unswapped:
                pieces += [piece, moved(piece, swap)]
            unswapped = []
        if step == half - 1:
            sums = far_part("far_part", first[: 4 * half - 5], block, number.shape[0], query_norm, sums, pieces)
            (below, above), sums = after([below, above], sums)
            below, above, keys, values = lax.optimization_barrier((below, above, below[:blocks], above[blocks:]))
            pieces = [above, moved(above, swap), below, moved(below, swap)]
    keys, values = moved(keys, up), moved(values, down)
    most = 2 * number.shape[0] // count
    sums = far_part("far_next", first[4 * half - 6 : 4 * half - 1], block, 4 * most, query_norm, sums, pieces)
    (keys, values), sums = after([keys, values], sums)
    pieces = [keys, moved(keys, swap), values, moved(values, swap)]
    return far_part("far_last", first[4 * half - 2 :], block, 2 * most, query_norm, sums, pieces, live)


def solution(mesh):
    in_specs = (
        P("tile", "head"),
        P("tile", "head"),
        P("tile", "head"),
        P("head"),
        P("head"),
        P("tile", None, "head"),
        P("tile", None, "head"),
        P("tile"),
        P("tile"),
        P("tile", None),
        P("tile"),
    )
    out_specs = P("tile", "head")
    return jax.shard_map(
        per_device, mesh=mesh, in_specs=in_specs, out_specs=out_specs, check_vma=False
    )
```

```python
import functools
import math

import jax
import jax.numpy as jnp
from jax import lax
from jax.experimental import pallas as pl
from jax.experimental.pallas import tpu as pltpu
from jax.sharding import PartitionSpec as P

HEAD_DIM = 128
WIDTH = 5120
EDGE = 64
EPSILON = 1e-06
HIDDEN = -1e30
VMEM_BYTES = 32 * 1024 * 1024


def passed_along(value, axis, steps):
    count = lax.axis_size(axis)
    first, last = (max(0, -steps), min(count, count - steps))
    return lax.ppermute(value, axis, [(source, source + steps) for source in range(first, last)])


def row_squares(raw_rows):
    rows32 = raw_rows.astype(jnp.float32)
    return jnp.sum(rows32 * rows32, axis=1)


def normalize(raw_rows, totals, gain):
    rows32 = raw_rows.astype(jnp.float32)
    factor = lax.rsqrt(totals / WIDTH + EPSILON)
    return (rows32 * factor[:, None] * gain).astype(jnp.bfloat16)


def chip_position(tile, levels):
    level, row = tile // 4, (tile // 2) % 2
    return level + row * (2 * levels - 1 - 2 * level)


def ring_pairs(count, step):
    levels = count // 4
    at = {(chip_position(t, levels), t % 2): t for t in range(count)}
    places = 2 * levels
    return [(at[p, c], at[(p + step) % places, c]) for p in range(places) for c in range(2)]


def across_t(first, second):
    return lax.dot_general(first, second, (((1,), (1,)), ((), ())), preferred_element_type=jnp.float32)


def down_rows(first, second):
    return lax.dot_general(first, second, (((0,), (0,)), ((), ())), preferred_element_type=jnp.float32)


def attend(heads):
    scores = []
    for query, parts, _ in heads:
        wide = [jnp.concatenate([bias] * (query.shape[0] // bias.shape[1]), axis=1) for _, _, bias in parts]
        scores.append([across_t(keys, query) + add for (keys, _, _), add in zip(parts, wide)])
    tops = []
    for group, (_, _, before) in zip(scores, heads):
        found = [jnp.max(part, axis=0, keepdims=True) for part in group]
        tops.append(functools.reduce(jnp.maximum, found if before is None else found + [before[0]]))
    weights = [[jnp.exp2(part - top) for part in group] for group, top in zip(scores, tops)]
    results = []
    for group, top, (_, parts, before) in zip(weights, tops, heads):
        total = sum(jnp.sum(part, axis=0, keepdims=True) for part in group)
        acc = sum(down_rows(values, part.astype(jnp.bfloat16)) for part, (_, values, _) in zip(group, parts))
        if before is not None:
            kept = jnp.exp2(before[0] - top)
            total = total + kept * before[1]
            acc = acc + kept * before[2]
        results.append((top, total, acc))
    return results


def store_sums(sums, head, place, top_ref, sum_ref, acc_ref):
    top, total, acc = sums
    top_ref[head] = jnp.broadcast_to(top, top_ref.shape[1:])
    sum_ref[head] = jnp.broadcast_to(total, sum_ref.shape[1:])
    acc_ref[place, :] = acc


def over_heads(width, body):
    heads = width // HEAD_DIM
    together = max(n for n in (1, 2, 4, 5) if heads % n == 0 and (n < 5 or heads < 10))

    def some(i, carry):
        numbers = [i * together + j for j in range(together)]
        body([(head, pl.ds(pl.multiple_of(head * HEAD_DIM, HEAD_DIM), HEAD_DIM)) for head in numbers])
        return carry

    lax.fori_loop(0, heads // together, some, 0)


def near_kernel(bias_ref, q_ref, k_ref, v_ref, ek_ref, ev_ref, top_ref, sum_ref, acc_ref):
    own = k_ref.shape[0]

    def body(places):
        heads = []
        for _, place in places:
            parts = [
                (k_ref[:, place], v_ref[:, place], bias_ref[:own, :]),
                (ek_ref[:, place], ev_ref[:, place], bias_ref[own:, :]),
            ]
            heads.append((q_ref[:, place], parts, None))
        for (head, place), sums in zip(places, attend(heads)):
            store_sums(sums, head, place, top_ref, sum_ref, acc_ref)

    over_heads(q_ref.shape[1], body)


def sum_shapes(rows, width):
    stat = jax.ShapeDtypeStruct((width // HEAD_DIM, 8, rows), jnp.float32)
    return [stat, stat, jax.ShapeDtypeStruct((width, rows), jnp.float32)]


IN_VMEM = pl.BlockSpec(memory_space=pltpu.VMEM)


def cost(rows, seen, width):
    return pl.CostEstimate(
        flops=4 * rows * seen * width,
        bytes_accessed=10 * rows * width,
        transcendentals=rows * seen * width // HEAD_DIM,
    )


def near_part(bias, query, keys, values, edge_keys, edge_values):
    rows, width = query.shape
    return pl.pallas_call(
        near_kernel,
        in_specs=[IN_VMEM] * 6,
        out_specs=[IN_VMEM] * 3,
        out_shape=sum_shapes(rows, width),
        compiler_params=pltpu.CompilerParams(vmem_limit_bytes=VMEM_BYTES),
        cost_estimate=cost(rows, bias.shape[0], width),
        name="near_part",
    )(bias, query, keys, values, edge_keys, edge_values)


def pick_kernel(groups, slots, first_ref, block_ref, *refs):
    key_pieces, value_pieces = refs[:groups], refs[groups : 2 * groups]
    picked, sem = refs[2 * groups :]
    start = first_ref[0]

    def fetch_from(g):
        def fetch(slot, carry):
            block = block_ref[slot]
            to = slot - start
            pltpu.make_async_copy(key_pieces[g].at[block], picked.at[to], sem).start()
            pltpu.make_async_copy(value_pieces[g].at[block], picked.at[slots + to], sem).start()
            return carry

        return fetch

    for g in range(groups):
        lax.fori_loop(first_ref[g], first_ref[g + 1], fetch_from(g), 0)
    lax.fori_loop(first_ref[groups], start + slots, fetch_from(0), 0)
    pltpu.make_async_copy(picked, picked, sem).wait()


def pick_part(name, first, block, slots, key_pieces, value_pieces):
    groups, (_, tokens, width) = len(key_pieces), key_pieces[0].shape
    block = jnp.concatenate([block, jnp.zeros((slots,), jnp.int32)])
    return pl.pallas_call(
        functools.partial(pick_kernel, groups, slots),
        in_specs=[pl.BlockSpec(memory_space=pltpu.SMEM)] * 2 + [pl.BlockSpec(memory_space=pl.ANY)] * (2 * groups),
        out_specs=pl.BlockSpec(memory_space=pl.ANY),
        out_shape=jax.ShapeDtypeStruct((2 * slots, tokens, width), jnp.bfloat16),
        scratch_shapes=[pltpu.SemaphoreType.DMA],
        cost_estimate=pl.CostEstimate(flops=0, bytes_accessed=8 * slots * tokens * width, transcendentals=0),
        name=name,
    )(first, block, *key_pieces, *value_pieces)


def far_kernel(groups, last, *refs):
    first_ref, block_ref, bias_ref, q_ref, before_top, before_sum, before_acc = refs[:7]
    refs = refs[7:]
    if last:
        live_ref, refs = refs[0], refs[1:]
    key_pieces, value_pieces, received = refs[:groups], refs[groups : 2 * groups], refs[2 * groups]
    *out_refs, keys, values, sems = refs[2 * groups + 1 :]
    slots, tokens = keys.shape[:2]
    offset = received.shape[0] // 2
    start = first_ref[0]

    def fetch_one(key_block, value_block, to):
        pltpu.make_async_copy(key_block, keys.at[to], sems.at[0]).start()
        pltpu.make_async_copy(value_block, values.at[to], sems.at[1]).start()

    def fetch_from(g):
        def fetch(slot, carry):
            block = block_ref[slot]
            fetch_one(key_pieces[g].at[block], value_pieces[g].at[block], slot - start)
            return carry

        return fetch

    def fetch_received(slot, carry):
        block = slot - first_ref[groups]
        fetch_one(received.at[block], received.at[offset + block], slot - start)
        return carry

    for g in range(groups):
        lax.fori_loop(first_ref[g], first_ref[g + 1], fetch_from(g), 0)
    lax.fori_loop(first_ref[groups], first_ref[groups + 1], fetch_received, 0)
    lax.fori_loop(first_ref[groups + 1], start + slots, fetch_from(0), 0)
    pltpu.make_async_copy(keys, keys, sems.at[0]).wait()
    pltpu.make_async_copy(values, values, sems.at[1]).wait()

    def flat(array, place):
        block = array[:, :, place].astype(jnp.float32)
        return block.reshape(slots * tokens, HEAD_DIM).astype(jnp.bfloat16)

    def body(places):
        heads = []
        for head, place in places:
            before = (before_top[head][:1, :], before_sum[head][:1, :], before_acc[place, :])
            heads.append((q_ref[:, place], [(flat(keys, place), flat(values, place), bias_ref[...])], before))
        for (head, place), sums in zip(places, attend(heads)):
            if last:
                result = jnp.where(live_ref[...] > 0.0, sums[2] / sums[1], 0.0)
                out_refs[0][:, place] = result.T.astype(out_refs[0].dtype)
            else:
                store_sums(sums, head, place, *out_refs)

    over_heads(q_ref.shape[1], body)


def far_part(name, first, block, slots, query, before, key_pieces, value_pieces, received, live=None):
    rows, width = query.shape
    groups, tokens = len(key_pieces), key_pieces[0].shape[1]
    seen = slots * tokens
    token = jnp.arange(seen, dtype=jnp.int32)[:, None]
    bias = jnp.where(token < (first[-1] - first[0]) * tokens, 0.0, jnp.float32(HIDDEN))
    bias = jnp.broadcast_to(bias, (seen, 128))
    block = jnp.concatenate([block, jnp.zeros((slots,), jnp.int32)])
    extra = [] if live is None else [live]
    final = jax.ShapeDtypeStruct((rows, width), jnp.bfloat16)
    return pl.pallas_call(
        functools.partial(far_kernel, groups, live is not None),
        in_specs=[pl.BlockSpec(memory_space=pltpu.SMEM)] * 2
        + [IN_VMEM] * (5 + len(extra))
        + [pl.BlockSpec(memory_space=pl.ANY)] * (2 * groups + 1),
        out_specs=[IN_VMEM] * 3 if live is None else IN_VMEM,
        out_shape=sum_shapes(rows, width) if live is None else final,
        input_output_aliases={4: 0, 5: 1, 6: 2} if live is None else {},
        scratch_shapes=[
            pltpu.VMEM((slots, tokens, width), jnp.bfloat16),
            pltpu.VMEM((slots, tokens, width), jnp.bfloat16),
            pltpu.SemaphoreType.DMA((2,)),
        ],
        compiler_params=pltpu.CompilerParams(vmem_limit_bytes=VMEM_BYTES),
        cost_estimate=cost(rows, seen, width),
        name=name,
    )(first, block, bias, query, *before, *extra, *key_pieces, *value_pieces, received)


def in_order(request, lane, owner_blocks, count, me):
    levels = count // 4
    places = 2 * levels
    half = places // 2
    owners, index = request // owner_blocks, request % owner_blocks
    ahead = (chip_position(owners, levels) - chip_position(me, levels)) % places
    distance = jnp.minimum(ahead, places - ahead)
    piece = jnp.where(distance == 0, 0, 2 * distance - 1 + (ahead > half).astype(jnp.int32))
    other = ((owners % 2) != lane).astype(jnp.int32)
    low, size = jnp.zeros_like(piece), jnp.zeros_like(piece)
    for first, stop in stages(half):
        inside = (piece >= first) & (piece < stop)
        low, size = jnp.where(inside, first, low), jnp.where(inside, stop - first, size)
    group = low + other * size + piece
    number = jnp.arange(group.shape[0], dtype=jnp.int32)
    rank_key = group * group.shape[0] + number
    rank = jnp.sum((rank_key[None, :] < rank_key[:, None]).astype(jnp.int32), axis=1)
    block = jnp.sum(jnp.where(rank[None, :] == number[:, None], index[None, :], 0), axis=1)
    groups = jnp.arange(2 * places + 1, dtype=jnp.int32)
    first = jnp.sum((group[None, :] < groups[:, None]).astype(jnp.int32), axis=1)
    return block, first


def stages(half):
    return (0, 2 * half - 3), (2 * half - 3, 2 * half - 1), (2 * half - 1, 2 * half)


def per_device(
    query_rows,
    key_rows,
    value_rows,
    gain_q,
    gain_k,
    mem_keys,
    mem_values,
    tile_len,
    session,
    req_owner,
    requested_block_index,
):
    capacity, width_here = query_rows.shape
    count = lax.axis_size("tile")
    levels = count // 4
    places = 2 * levels
    half = places // 2
    me = lax.axis_index("tile")

    swap = [(t, t ^ 1) for t in range(count)]
    owner_blocks = mem_keys.shape[0]
    request = req_owner[:, 0] * owner_blocks + requested_block_index
    my_block, my_first = in_order(request, me % 2, owner_blocks, count, me)
    my_plan = jnp.concatenate([my_first, my_block])

    my_length = tile_len[0]
    totals_q, totals_k = lax.psum((row_squares(query_rows), row_squares(key_rows)), "head")
    query_norm = normalize(query_rows, totals_q, gain_q * (math.log2(math.e) / HEAD_DIM**0.5))
    key_norm = normalize(key_rows, totals_k, gain_k)
    live_rows = jnp.arange(capacity, dtype=jnp.int32) < my_length
    live = live_rows[None, :].astype(jnp.float32)
    own_label = (session[0] + 1).astype(jnp.bfloat16)
    edge_index = jnp.arange(EDGE, dtype=jnp.int32)
    blank = jnp.zeros((EDGE, width_here), jnp.bfloat16)

    def tail(rows):
        return lax.dynamic_slice_in_dim(jnp.concatenate([blank, rows], 0), my_length, EDGE, 0)

    def edge(keys, values, is_live):
        labels = jnp.where(is_live, own_label, jnp.bfloat16(0))
        return jnp.concatenate([keys, values, jnp.pad(labels[None, :], ((0, 15), (0, width_here - EDGE)))], 0)

    tails = edge(tail(key_norm), tail(value_rows), edge_index >= EDGE - my_length)
    fronts = edge(key_norm[:EDGE], value_rows[:EDGE], edge_index < my_length)
    from_left, from_right = passed_along(tails, "tile", 1), passed_along(fronts, "tile", -1)

    def near_sums(from_left, from_right):
        edge_keys = jnp.concatenate([from_left[:EDGE], from_right[:EDGE]], 0)
        edge_values = jnp.concatenate([from_left[EDGE : 2 * EDGE], from_right[EDGE : 2 * EDGE]], 0)
        labels = jnp.concatenate([from_left[2 * EDGE, :EDGE], from_right[2 * EDGE, :EDGE]])
        bias = jnp.where(jnp.concatenate([live_rows, labels == own_label]), 0.0, jnp.float32(HIDDEN))
        bias = jnp.broadcast_to(bias[:, None], (bias.shape[0], 128))
        return near_part(bias, query_norm, key_norm, value_rows, edge_keys, edge_values)

    up, down = ring_pairs(count, 1), ring_pairs(count, -1)

    def moved(piece, pairs):
        return lax.ppermute(piece, "tile", pairs)

    def after(pieces, results):
        *pieces, top = lax.optimization_barrier((*pieces, results[0]))
        return pieces, [top, *results[1:]]

    keys, values = [mem_keys], [mem_values]
    for step in range(1, half):
        for pieces in (keys, values):
            pieces += [moved(pieces[-2 if step > 1 else -1], down), moved(pieces[-1], up)]
        if step == 1:
            from_left, from_right, *_ = lax.optimization_barrier((from_left, from_right, *values[1:]))
            sums = near_sums(from_left, from_right)
    keys.append(moved(keys[-1], up))
    values.append(moved(values[-2], down))

    most = 2 * request.shape[0] // count
    limits = (min(request.shape[0], count * most), 2 * most, most)
    for stage, ((first, stop), limit) in enumerate(zip(stages(half), limits)):
        name = ("first", "second", "third")[stage]
        size = stop - first
        (*pieces,), sums = after([*keys[first:stop], *values[first:stop]], sums)
        plan, *pieces = lax.optimization_barrier((my_plan, *pieces))
        plan = moved(plan, swap)
        their_first, their_block = plan[: my_first.shape[0]], plan[my_first.shape[0] :]
        key_pieces, value_pieces = pieces[:size], pieces[size:]
        theirs = their_first[2 * first + size : 2 * stop + 1]
        picked = pick_part("pick_" + name, theirs, their_block, limit, key_pieces, value_pieces)
        mine = jnp.concatenate([my_first[2 * first : 2 * first + size + 1], my_first[2 * stop :][:1]])
        sums = far_part(
            "far_" + name,
            mine,
            my_block,
            min(request.shape[0], 2 * limit),
            query_norm,
            sums,
            key_pieces,
            value_pieces,
            moved(picked, swap),
            live if stage == 2 else None,
        )
    return sums


def solution(mesh):
    in_specs = (
        P("tile", "head"),
        P("tile", "head"),
        P("tile", "head"),
        P("head"),
        P("head"),
        P("tile", None, "head"),
        P("tile", None, "head"),
        P("tile"),
        P("tile"),
        P("tile", None),
        P("tile"),
    )
    out_specs = P("tile", "head")
    return jax.shard_map(
        per_device, mesh=mesh, in_specs=in_specs, out_specs=out_specs, check_vma=False
    )
```

```python
import functools
import math

import jax
import jax.numpy as jnp
from jax import lax
from jax.experimental import pallas as pl
from jax.experimental.pallas import tpu as pltpu
from jax.sharding import PartitionSpec as P

HEAD_DIM = 128
WIDTH = 5120
EDGE = 64
EPSILON = 1e-06
HIDDEN = -1e30
VMEM_BYTES = 24 * 1024 * 1024


def passed_along(value, axis, steps):
    count = lax.axis_size(axis)
    first, last = (max(0, -steps), min(count, count - steps))
    return lax.ppermute(value, axis, [(source, source + steps) for source in range(first, last)])


def row_squares(raw_rows):
    rows32 = raw_rows.astype(jnp.float32)
    return jnp.sum(rows32 * rows32, axis=1)


def normalize(raw_rows, totals, gain):
    rows32 = raw_rows.astype(jnp.float32)
    factor = lax.rsqrt(totals / WIDTH + EPSILON)
    return (rows32 * factor[:, None] * gain).astype(jnp.bfloat16)


def chip_position(tile, levels):
    level, row = tile // 4, (tile // 2) % 2
    return level + row * (2 * levels - 1 - 2 * level)


def ring_pairs(count, step):
    levels = count // 4
    at = {(chip_position(t, levels), t % 2): t for t in range(count)}
    places = 2 * levels
    return [(at[p, c], at[(p + step) % places, c]) for p in range(places) for c in range(2)]


def across_t(first, second):
    return lax.dot_general(first, second, (((1,), (1,)), ((), ())), preferred_element_type=jnp.float32)


def down_rows(first, second):
    return lax.dot_general(first, second, (((0,), (0,)), ((), ())), preferred_element_type=jnp.float32)


def attend(heads):
    scores = []
    for query, parts, _ in heads:
        wide = [jnp.concatenate([bias] * (query.shape[0] // bias.shape[1]), axis=1) for _, _, bias in parts]
        scores.append([across_t(keys, query) + add for (keys, _, _), add in zip(parts, wide)])
    tops = []
    for group, (_, _, before) in zip(scores, heads):
        found = [jnp.max(part, axis=0, keepdims=True) for part in group]
        tops.append(functools.reduce(jnp.maximum, found if before is None else found + [before[0]]))
    weights = [[jnp.exp2(part - top) for part in group] for group, top in zip(scores, tops)]
    results = []
    for group, top, (_, parts, before) in zip(weights, tops, heads):
        total = sum(jnp.sum(part, axis=0, keepdims=True) for part in group)
        acc = sum(down_rows(values, part.astype(jnp.bfloat16)) for part, (_, values, _) in zip(group, parts))
        if before is not None:
            kept = jnp.exp2(before[0] - top)
            total = total + kept * before[1]
            acc = acc + kept * before[2]
        results.append((top, total, acc))
    return results


def store_sums(sums, head, place, top_ref, sum_ref, acc_ref):
    top, total, acc = sums
    top_ref[head] = jnp.broadcast_to(top, top_ref.shape[1:])
    sum_ref[head] = jnp.broadcast_to(total, sum_ref.shape[1:])
    acc_ref[place, :] = acc


def over_heads(width, body):
    heads = width // HEAD_DIM
    together = max(n for n in (1, 2, 4, 5) if heads % n == 0 and (n < 5 or heads < 10))

    def some(i, carry):
        numbers = [i * together + j for j in range(together)]
        body([(head, pl.ds(pl.multiple_of(head * HEAD_DIM, HEAD_DIM), HEAD_DIM)) for head in numbers])
        return carry

    lax.fori_loop(0, heads // together, some, 0)


def near_kernel(bias_ref, q_ref, k_ref, v_ref, ek_ref, ev_ref, top_ref, sum_ref, acc_ref):
    own = k_ref.shape[0]

    def body(places):
        heads = []
        for _, place in places:
            parts = [
                (k_ref[:, place], v_ref[:, place], bias_ref[:own, :]),
                (ek_ref[:, place], ev_ref[:, place], bias_ref[own:, :]),
            ]
            heads.append((q_ref[:, place], parts, None))
        for (head, place), sums in zip(places, attend(heads)):
            store_sums(sums, head, place, top_ref, sum_ref, acc_ref)

    over_heads(q_ref.shape[1], body)


def sum_shapes(rows, width):
    stat = jax.ShapeDtypeStruct((width // HEAD_DIM, 8, rows), jnp.float32)
    return [stat, stat, jax.ShapeDtypeStruct((width, rows), jnp.float32)]


IN_VMEM = pl.BlockSpec(memory_space=pltpu.VMEM)
IN_HBM = pl.BlockSpec(memory_space=pltpu.HBM)


def cost(rows, seen, width):
    return pl.CostEstimate(
        flops=4 * rows * seen * width,
        bytes_accessed=10 * rows * width,
        transcendentals=rows * seen * width // HEAD_DIM,
    )


def near_part(bias, query, keys, values, edge_keys, edge_values):
    rows, width = query.shape
    return pl.pallas_call(
        near_kernel,
        in_specs=[IN_VMEM] * 6,
        out_specs=[IN_VMEM] * 3,
        out_shape=sum_shapes(rows, width),
        compiler_params=pltpu.CompilerParams(vmem_limit_bytes=VMEM_BYTES),
        cost_estimate=cost(rows, bias.shape[0], width),
        name="near_part",
    )(bias, query, keys, values, edge_keys, edge_values)


def pick_kernel(groups, slots, first_ref, block_ref, *refs):
    key_pieces, value_pieces = refs[:groups], refs[groups : 2 * groups]
    picked, sem = refs[2 * groups :]
    start = first_ref[0]

    def fetch_from(g):
        def fetch(slot, carry):
            block = block_ref[slot]
            to = slot - start
            pltpu.make_async_copy(key_pieces[g].at[block], picked.at[to], sem).start()
            pltpu.make_async_copy(value_pieces[g].at[block], picked.at[slots + to], sem).start()
            return carry

        return fetch

    for g in range(groups):
        lax.fori_loop(first_ref[g], first_ref[g + 1], fetch_from(g), 0)
    lax.fori_loop(first_ref[groups], start + slots, fetch_from(0), 0)
    pltpu.make_async_copy(picked, picked, sem).wait()


def pick_part(name, first, block, slots, key_pieces, value_pieces):
    groups, (_, tokens, width) = len(key_pieces), key_pieces[0].shape
    block = jnp.concatenate([block, jnp.zeros((slots,), jnp.int32)])
    return pl.pallas_call(
        functools.partial(pick_kernel, groups, slots),
        in_specs=[pl.BlockSpec(memory_space=pltpu.SMEM)] * 2 + [IN_HBM] * (2 * groups),
        out_specs=IN_VMEM,
        out_shape=jax.ShapeDtypeStruct((2 * slots, tokens, width), jnp.bfloat16),
        scratch_shapes=[pltpu.SemaphoreType.DMA],
        compiler_params=pltpu.CompilerParams(vmem_limit_bytes=VMEM_BYTES),
        cost_estimate=pl.CostEstimate(flops=0, bytes_accessed=8 * slots * tokens * width, transcendentals=0),
        name=name,
    )(first, block, *key_pieces, *value_pieces)


def far_kernel(groups, last, *refs):
    first_ref, block_ref, bias_ref, q_ref, before_top, before_sum, before_acc = refs[:7]
    refs = refs[7:]
    if last:
        live_ref, refs = refs[0], refs[1:]
    key_pieces, value_pieces, received = refs[:groups], refs[groups : 2 * groups], refs[2 * groups]
    *out_refs, keys, values, sems = refs[2 * groups + 1 :]
    slots, tokens = keys.shape[:2]
    offset = received.shape[0] // 2
    start = first_ref[0]

    def fetch_one(key_block, value_block, to):
        pltpu.make_async_copy(key_block, keys.at[to], sems.at[0]).start()
        pltpu.make_async_copy(value_block, values.at[to], sems.at[1]).start()

    def fetch_from(g):
        def fetch(slot, carry):
            block = block_ref[slot]
            fetch_one(key_pieces[g].at[block], value_pieces[g].at[block], slot - start)
            return carry

        return fetch

    def fetch_received(slot, carry):
        block = slot - first_ref[groups]
        fetch_one(received.at[block], received.at[offset + block], slot - start)
        return carry

    for g in range(groups):
        lax.fori_loop(first_ref[g], first_ref[g + 1], fetch_from(g), 0)
    lax.fori_loop(first_ref[groups], first_ref[groups + 1], fetch_received, 0)
    lax.fori_loop(first_ref[groups + 1], start + slots, fetch_from(0), 0)
    pltpu.make_async_copy(keys, keys, sems.at[0]).wait()
    pltpu.make_async_copy(values, values, sems.at[1]).wait()

    def flat(array, place):
        block = array[:, :, place].astype(jnp.float32)
        return block.reshape(slots * tokens, HEAD_DIM).astype(jnp.bfloat16)

    def body(places):
        heads = []
        for head, place in places:
            before = (before_top[head][:1, :], before_sum[head][:1, :], before_acc[place, :])
            heads.append((q_ref[:, place], [(flat(keys, place), flat(values, place), bias_ref[...])], before))
        for (head, place), sums in zip(places, attend(heads)):
            if last:
                result = jnp.where(live_ref[...] > 0.0, sums[2] / sums[1], 0.0)
                out_refs[0][:, place] = result.T.astype(out_refs[0].dtype)
            else:
                store_sums(sums, head, place, *out_refs)

    over_heads(q_ref.shape[1], body)


def far_part(name, first, block, slots, query, before, key_pieces, value_pieces, received, live=None):
    rows, width = query.shape
    groups, tokens = len(key_pieces), key_pieces[0].shape[1]
    seen = slots * tokens
    token = jnp.arange(seen, dtype=jnp.int32)[:, None]
    bias = jnp.where(token < (first[-1] - first[0]) * tokens, 0.0, jnp.float32(HIDDEN))
    bias = jnp.broadcast_to(bias, (seen, 128))
    block = jnp.concatenate([block, jnp.zeros((slots,), jnp.int32)])
    extra = [] if live is None else [live]
    final = jax.ShapeDtypeStruct((rows, width), jnp.bfloat16)
    return pl.pallas_call(
        functools.partial(far_kernel, groups, live is not None),
        in_specs=[pl.BlockSpec(memory_space=pltpu.SMEM)] * 2
        + [IN_VMEM] * (5 + len(extra))
        + [IN_HBM] * (2 * groups + 1),
        out_specs=[IN_VMEM] * 3 if live is None else IN_VMEM,
        out_shape=sum_shapes(rows, width) if live is None else final,
        input_output_aliases={4: 0, 5: 1, 6: 2} if live is None else {},
        scratch_shapes=[
            pltpu.VMEM((slots, tokens, width), jnp.bfloat16),
            pltpu.VMEM((slots, tokens, width), jnp.bfloat16),
            pltpu.SemaphoreType.DMA((2,)),
        ],
        compiler_params=pltpu.CompilerParams(vmem_limit_bytes=VMEM_BYTES),
        cost_estimate=cost(rows, seen, width),
        name=name,
    )(first, block, bias, query, *before, *extra, *key_pieces, *value_pieces, received)


def in_order(request, lane, owner_blocks, count, me):
    levels = count // 4
    places = 2 * levels
    half = places // 2
    owners, index = request // owner_blocks, request % owner_blocks
    ahead = (chip_position(owners, levels) - chip_position(me, levels)) % places
    distance = jnp.minimum(ahead, places - ahead)
    piece = jnp.where(distance == 0, 0, 2 * distance - 1 + (ahead > half).astype(jnp.int32))
    other = ((owners % 2) != lane).astype(jnp.int32)
    low, size = jnp.zeros_like(piece), jnp.zeros_like(piece)
    for first, stop in stages(half):
        inside = (piece >= first) & (piece < stop)
        low, size = jnp.where(inside, first, low), jnp.where(inside, stop - first, size)
    group = low + other * size + piece
    number = jnp.arange(group.shape[0], dtype=jnp.int32)
    rank_key = group * group.shape[0] + number
    rank = jnp.sum((rank_key[None, :] < rank_key[:, None]).astype(jnp.int32), axis=1)
    block = jnp.sum(jnp.where(rank[None, :] == number[:, None], index[None, :], 0), axis=1)
    groups = jnp.arange(2 * places + 1, dtype=jnp.int32)
    first = jnp.sum((group[None, :] < groups[:, None]).astype(jnp.int32), axis=1)
    return block, first


def stages(half):
    return (0, 2 * half - 3), (2 * half - 3, 2 * half - 1), (2 * half - 1, 2 * half)


def per_device(
    query_rows,
    key_rows,
    value_rows,
    gain_q,
    gain_k,
    mem_keys,
    mem_values,
    tile_len,
    session,
    req_owner,
    requested_block_index,
):
    capacity, width_here = query_rows.shape
    count = lax.axis_size("tile")
    levels = count // 4
    places = 2 * levels
    half = places // 2
    me = lax.axis_index("tile")

    swap = [(t, t ^ 1) for t in range(count)]
    owner_blocks = mem_keys.shape[0]
    request = req_owner[:, 0] * owner_blocks + requested_block_index
    my_block, my_first = in_order(request, me % 2, owner_blocks, count, me)
    plan = lax.ppermute(jnp.concatenate([my_first, my_block]), "tile", swap)
    their_first, their_block = plan[: my_first.shape[0]], plan[my_first.shape[0] :]

    my_length = tile_len[0]
    live_rows = jnp.arange(capacity, dtype=jnp.int32) < my_length
    live = live_rows[None, :].astype(jnp.float32)
    own_label = (session[0] + 1).astype(jnp.bfloat16)
    edge_index = jnp.arange(EDGE, dtype=jnp.int32)
    blank = jnp.zeros((EDGE, width_here), jnp.bfloat16)

    def tail(rows):
        return lax.dynamic_slice_in_dim(jnp.concatenate([blank, rows], 0), my_length, EDGE, 0)

    def edge(keys, values, is_live):
        labels = jnp.where(is_live, own_label, jnp.bfloat16(0))
        return jnp.concatenate([keys, values, jnp.pad(labels[None, :], ((0, 15), (0, width_here - EDGE)))], 0)

    tails = edge(tail(key_rows), tail(value_rows), edge_index >= EDGE - my_length)
    fronts = edge(key_rows[:EDGE], value_rows[:EDGE], edge_index < my_length)
    from_left, from_right = passed_along(tails, "tile", 1), passed_along(fronts, "tile", -1)
    from_left, from_right, mem_keys, mem_values = lax.optimization_barrier(
        (from_left, from_right, mem_keys, mem_values)
    )

    edge_keys = jnp.concatenate([from_left[:EDGE], from_right[:EDGE]], 0)
    edge_values = jnp.concatenate([from_left[EDGE : 2 * EDGE], from_right[EDGE : 2 * EDGE]], 0)
    labels = jnp.concatenate([from_left[2 * EDGE, :EDGE], from_right[2 * EDGE, :EDGE]])
    totals_q, totals_k, totals_e = lax.psum(
        (row_squares(query_rows), row_squares(key_rows), row_squares(edge_keys)), "head"
    )
    query_norm = normalize(query_rows, totals_q, gain_q * (math.log2(math.e) / HEAD_DIM**0.5))
    key_norm = normalize(key_rows, totals_k, gain_k)
    edge_norm = normalize(edge_keys, totals_e, gain_k)
    bias = jnp.where(jnp.concatenate([live_rows, labels == own_label]), 0.0, jnp.float32(HIDDEN))
    bias = jnp.broadcast_to(bias[:, None], (bias.shape[0], 128))
    sums = near_part(bias, query_norm, key_norm, value_rows, edge_norm, edge_values)

    up, down = ring_pairs(count, 1), ring_pairs(count, -1)

    def moved(piece, pairs):
        return lax.ppermute(piece, "tile", pairs)

    def after(pieces, results):
        *pieces, top = lax.optimization_barrier((*pieces, results[0]))
        return pieces, [top, *results[1:]]

    keys, values = [mem_keys], [mem_values]
    for step in range(1, half):
        for pieces in (keys, values):
            pieces += [moved(pieces[-2 if step > 1 else -1], down), moved(pieces[-1], up)]
    keys.append(moved(keys[-1], up))
    values.append(moved(values[-2], down))

    most = 2 * request.shape[0] // count
    limits = (min(request.shape[0], count * most), 2 * most, most)
    for stage, ((first, stop), limit) in enumerate(zip(stages(half), limits)):
        name = ("first", "second", "third")[stage]
        size = stop - first
        (*pieces,), sums = after([*keys[first:stop], *values[first:stop]], sums)
        key_pieces, value_pieces = pieces[:size], pieces[size:]
        theirs = their_first[2 * first + size : 2 * stop + 1]
        picked = pick_part("pick_" + name, theirs, their_block, limit, key_pieces, value_pieces)
        mine = jnp.concatenate([my_first[2 * first : 2 * first + size + 1], my_first[2 * stop :][:1]])
        sums = far_part(
            "far_" + name,
            mine,
            my_block,
            min(request.shape[0], 2 * limit),
            query_norm,
            sums,
            key_pieces,
            value_pieces,
            moved(picked, swap),
            live if stage == 2 else None,
        )
    return sums


def solution(mesh):
    in_specs = (
        P("tile", "head"),
        P("tile", "head"),
        P("tile", "head"),
        P("head"),
        P("head"),
        P("tile", None, "head"),
        P("tile", None, "head"),
        P("tile"),
        P("tile"),
        P("tile", None),
        P("tile"),
    )
    out_specs = P("tile", "head")
    return jax.shard_map(
        per_device, mesh=mesh, in_specs=in_specs, out_specs=out_specs, check_vma=False
    )
```

```python
import functools
import math

import jax
import jax.numpy as jnp
from jax import lax
from jax.experimental import pallas as pl
from jax.experimental.pallas import tpu as pltpu
from jax.sharding import PartitionSpec as P

HEAD_DIM = 128
WIDTH = 5120
EDGE = 64
EPSILON = 1e-06
HIDDEN = -1e30
VMEM_BYTES = 24 * 1024 * 1024


def passed_along(value, axis, steps):
    count = lax.axis_size(axis)
    first, last = (max(0, -steps), min(count, count - steps))
    return lax.ppermute(value, axis, [(source, source + steps) for source in range(first, last)])


def row_squares(raw_rows):
    rows32 = raw_rows.astype(jnp.float32)
    return jnp.sum(rows32 * rows32, axis=1)


def normalize(raw_rows, totals, gain):
    rows32 = raw_rows.astype(jnp.float32)
    factor = lax.rsqrt(totals / WIDTH + EPSILON)
    return (rows32 * factor[:, None] * gain).astype(jnp.bfloat16)


def chip_position(tile, levels):
    level, row = tile // 4, (tile // 2) % 2
    return level + row * (2 * levels - 1 - 2 * level)


def ring_pairs(count, step):
    levels = count // 4
    at = {(chip_position(t, levels), t % 2): t for t in range(count)}
    places = 2 * levels
    return [(at[p, c], at[(p + step) % places, c]) for p in range(places) for c in range(2)]


def across_t(first, second):
    return lax.dot_general(first, second, (((1,), (1,)), ((), ())), preferred_element_type=jnp.float32)


def down_rows(first, second):
    return lax.dot_general(first, second, (((0,), (0,)), ((), ())), preferred_element_type=jnp.float32)


def attend(heads):
    scores = []
    for query, parts, _ in heads:
        wide = [jnp.concatenate([bias] * (query.shape[0] // bias.shape[1]), axis=1) for _, _, bias in parts]
        scores.append([across_t(keys, query) + add for (keys, _, _), add in zip(parts, wide)])
    tops = []
    for group, (_, _, before) in zip(scores, heads):
        found = [jnp.max(part, axis=0, keepdims=True) for part in group]
        tops.append(functools.reduce(jnp.maximum, found if before is None else found + [before[0]]))
    weights = [[jnp.exp2(part - top) for part in group] for group, top in zip(scores, tops)]
    results = []
    for group, top, (_, parts, before) in zip(weights, tops, heads):
        total = sum(jnp.sum(part, axis=0, keepdims=True) for part in group)
        acc = sum(down_rows(values, part.astype(jnp.bfloat16)) for part, (_, values, _) in zip(group, parts))
        if before is not None:
            kept = jnp.exp2(before[0] - top)
            total = total + kept * before[1]
            acc = acc + kept * before[2]
        results.append((top, total, acc))
    return results


def store_sums(sums, head, place, top_ref, sum_ref, acc_ref):
    top, total, acc = sums
    top_ref[head] = jnp.broadcast_to(top, top_ref.shape[1:])
    sum_ref[head] = jnp.broadcast_to(total, sum_ref.shape[1:])
    acc_ref[place, :] = acc


def over_heads(width, body):
    heads = width // HEAD_DIM
    together = max(n for n in (1, 2, 4, 5) if heads % n == 0 and (n < 5 or heads < 10))

    def some(i, carry):
        numbers = [i * together + j for j in range(together)]
        body([(head, pl.ds(pl.multiple_of(head * HEAD_DIM, HEAD_DIM), HEAD_DIM)) for head in numbers])
        return carry

    lax.fori_loop(0, heads // together, some, 0)


def near_kernel(bias_ref, q_ref, k_ref, v_ref, ek_ref, ev_ref, top_ref, sum_ref, acc_ref):
    own = k_ref.shape[0]

    def body(places):
        heads = []
        for _, place in places:
            parts = [
                (k_ref[:, place], v_ref[:, place], bias_ref[:own, :]),
                (ek_ref[:, place], ev_ref[:, place], bias_ref[own:, :]),
            ]
            heads.append((q_ref[:, place], parts, None))
        for (head, place), sums in zip(places, attend(heads)):
            store_sums(sums, head, place, top_ref, sum_ref, acc_ref)

    over_heads(q_ref.shape[1], body)


def sum_shapes(rows, width):
    stat = jax.ShapeDtypeStruct((width // HEAD_DIM, 8, rows), jnp.float32)
    return [stat, stat, jax.ShapeDtypeStruct((width, rows), jnp.float32)]


IN_VMEM = pl.BlockSpec(memory_space=pltpu.VMEM)
IN_HBM = pl.BlockSpec(memory_space=pltpu.HBM)


def cost(rows, seen, width):
    return pl.CostEstimate(
        flops=4 * rows * seen * width,
        bytes_accessed=10 * rows * width,
        transcendentals=rows * seen * width // HEAD_DIM,
    )


def near_part(bias, query, keys, values, edge_keys, edge_values):
    rows, width = query.shape
    return pl.pallas_call(
        near_kernel,
        in_specs=[IN_VMEM] * 6,
        out_specs=[IN_VMEM] * 3,
        out_shape=sum_shapes(rows, width),
        compiler_params=pltpu.CompilerParams(vmem_limit_bytes=VMEM_BYTES),
        cost_estimate=cost(rows, bias.shape[0], width),
        name="near_part",
    )(bias, query, keys, values, edge_keys, edge_values)


def pick_kernel(groups, slots, first_ref, block_ref, *refs):
    key_pieces, value_pieces = refs[:groups], refs[groups : 2 * groups]
    picked, sem = refs[2 * groups :]
    start = first_ref[0]

    def fetch_from(g):
        def fetch(slot, carry):
            block = block_ref[slot]
            to = slot - start
            pltpu.make_async_copy(key_pieces[g].at[block], picked.at[to], sem).start()
            pltpu.make_async_copy(value_pieces[g].at[block], picked.at[slots + to], sem).start()
            return carry

        return fetch

    for g in range(groups):
        lax.fori_loop(first_ref[g], first_ref[g + 1], fetch_from(g), 0)
    lax.fori_loop(first_ref[groups], start + slots, fetch_from(0), 0)
    pltpu.make_async_copy(picked, picked, sem).wait()


def pick_part(name, first, block, slots, key_pieces, value_pieces):
    groups, (_, tokens, width) = len(key_pieces), key_pieces[0].shape
    block = jnp.concatenate([block, jnp.zeros((slots,), jnp.int32)])
    return pl.pallas_call(
        functools.partial(pick_kernel, groups, slots),
        in_specs=[pl.BlockSpec(memory_space=pltpu.SMEM)] * 2 + [IN_HBM] * (2 * groups),
        out_specs=IN_VMEM,
        out_shape=jax.ShapeDtypeStruct((2 * slots, tokens, width), jnp.bfloat16),
        scratch_shapes=[pltpu.SemaphoreType.DMA],
        compiler_params=pltpu.CompilerParams(vmem_limit_bytes=VMEM_BYTES),
        cost_estimate=pl.CostEstimate(flops=0, bytes_accessed=8 * slots * tokens * width, transcendentals=0),
        name=name,
    )(first, block, *key_pieces, *value_pieces)


def far_kernel(segments, last, beside, *refs):
    first_ref, block_ref, bias_ref, q_ref, before_top, before_sum, before_acc = refs[:7]
    refs = refs[7:]
    if last:
        live_ref, refs = refs[0], refs[1:]
    if beside:
        (beside_bias, beside_keys, beside_values), refs = refs[:3], refs[3:]
    *out_refs, keys, values, sems = refs[sum(2 * size + 1 for size in segments) :]
    slots, tokens = keys.shape[:2]
    start = first_ref[0]

    def fetch_one(key_block, value_block, to):
        pltpu.make_async_copy(key_block, keys.at[to], sems.at[0]).start()
        pltpu.make_async_copy(value_block, values.at[to], sems.at[1]).start()

    def fetch_from(key_piece, value_piece):
        def fetch(slot, carry):
            block = block_ref[slot]
            fetch_one(key_piece.at[block], value_piece.at[block], slot - start)
            return carry

        return fetch

    def fetch_received(received, base):
        def fetch(slot, carry):
            block = slot - base
            fetch_one(received.at[block], received.at[received.shape[0] // 2 + block], slot - start)
            return carry

        return fetch

    at, pieces = 0, refs
    for size in segments:
        for g in range(size):
            lax.fori_loop(first_ref[at], first_ref[at + 1], fetch_from(pieces[g], pieces[size + g]), 0)
            at += 1
        lax.fori_loop(first_ref[at], first_ref[at + 1], fetch_received(pieces[2 * size], first_ref[at]), 0)
        at += 1
        pieces = pieces[2 * size + 1 :]
    lax.fori_loop(first_ref[at], start + slots, fetch_from(refs[0], refs[segments[0]]), 0)
    pltpu.make_async_copy(keys, keys, sems.at[0]).wait()
    pltpu.make_async_copy(values, values, sems.at[1]).wait()

    def flat(array, place):
        block = array[:, :, place].astype(jnp.float32)
        return block.reshape(slots * tokens, HEAD_DIM).astype(jnp.bfloat16)

    def body(places):
        heads = []
        for head, place in places:
            before = (before_top[head][:1, :], before_sum[head][:1, :], before_acc[place, :])
            parts = [(flat(keys, place), flat(values, place), bias_ref[...])]
            if beside:
                parts.append((beside_keys[:, place], beside_values[:, place], beside_bias[...]))
            heads.append((q_ref[:, place], parts, before))
        for (head, place), sums in zip(places, attend(heads)):
            if last:
                result = jnp.where(live_ref[...] > 0.0, sums[2] / sums[1], 0.0)
                out_refs[0][:, place] = result.T.astype(out_refs[0].dtype)
            else:
                store_sums(sums, head, place, *out_refs)

    over_heads(q_ref.shape[1], body)


def far_part(name, first, block, slots, query, before, segments, live=None, beside=()):
    rows, width = query.shape
    pieces = [array for segment in segments for array in segment]
    tokens = pieces[0].shape[1]
    seen = slots * tokens
    token = jnp.arange(seen, dtype=jnp.int32)[:, None]
    bias = jnp.where(token < (first[-1] - first[0]) * tokens, 0.0, jnp.float32(HIDDEN))
    bias = jnp.broadcast_to(bias, (seen, 128))
    block = jnp.concatenate([block, jnp.zeros((slots,), jnp.int32)])
    extra = ([] if live is None else [live]) + list(beside)
    final = jax.ShapeDtypeStruct((rows, width), jnp.bfloat16)
    return pl.pallas_call(
        functools.partial(far_kernel, [len(segment) // 2 for segment in segments], live is not None, len(beside) > 0),
        in_specs=[pl.BlockSpec(memory_space=pltpu.SMEM)] * 2
        + [IN_VMEM] * (5 + len(extra))
        + [IN_HBM] * len(pieces),
        out_specs=[IN_VMEM] * 3 if live is None else IN_VMEM,
        out_shape=sum_shapes(rows, width) if live is None else final,
        input_output_aliases={4: 0, 5: 1, 6: 2} if live is None else {},
        scratch_shapes=[
            pltpu.VMEM((slots, tokens, width), jnp.bfloat16),
            pltpu.VMEM((slots, tokens, width), jnp.bfloat16),
            pltpu.SemaphoreType.DMA((2,)),
        ],
        compiler_params=pltpu.CompilerParams(vmem_limit_bytes=VMEM_BYTES),
        cost_estimate=cost(rows, seen, width),
        name=name,
    )(first, block, bias, query, *before, *extra, *pieces)


def in_order(request, lane, owner_blocks, count, me):
    levels = count // 4
    places = 2 * levels
    half = places // 2
    owners, index = request // owner_blocks, request % owner_blocks
    ahead = (chip_position(owners, levels) - chip_position(me, levels)) % places
    distance = jnp.minimum(ahead, places - ahead)
    piece = jnp.where(distance == 0, 0, 2 * distance - 1 + (ahead > half).astype(jnp.int32))
    other = ((owners % 2) != lane).astype(jnp.int32)
    low, size = jnp.zeros_like(piece), jnp.zeros_like(piece)
    for first, stop in stages(half):
        inside = (piece >= first) & (piece < stop)
        low, size = jnp.where(inside, first, low), jnp.where(inside, stop - first, size)
    group = low + other * size + piece
    number = jnp.arange(group.shape[0], dtype=jnp.int32)
    rank_key = group * group.shape[0] + number
    rank = jnp.sum((rank_key[None, :] < rank_key[:, None]).astype(jnp.int32), axis=1)
    block = jnp.sum(jnp.where(rank[None, :] == number[:, None], index[None, :], 0), axis=1)
    groups = jnp.arange(2 * places + 1, dtype=jnp.int32)
    first = jnp.sum((group[None, :] < groups[:, None]).astype(jnp.int32), axis=1)
    return block, first


def stages(half):
    return (0, 2 * half - 5), (2 * half - 5, 2 * half - 3), (2 * half - 3, 2 * half - 1), (2 * half - 1, 2 * half)


def per_device(
    query_rows,
    key_rows,
    value_rows,
    gain_q,
    gain_k,
    mem_keys,
    mem_values,
    tile_len,
    session,
    req_owner,
    requested_block_index,
):
    capacity, width_here = query_rows.shape
    count = lax.axis_size("tile")
    levels = count // 4
    places = 2 * levels
    half = places // 2
    me = lax.axis_index("tile")

    swap = [(t, t ^ 1) for t in range(count)]
    owner_blocks = mem_keys.shape[0]
    request = req_owner[:, 0] * owner_blocks + requested_block_index
    my_block, my_first = in_order(request, me % 2, owner_blocks, count, me)
    plan = lax.ppermute(jnp.concatenate([my_first, my_block]), "tile", swap)
    their_first, their_block = plan[: my_first.shape[0]], plan[my_first.shape[0] :]

    my_length = tile_len[0]
    totals_q, totals_k = lax.psum((row_squares(query_rows), row_squares(key_rows)), "head")
    query_norm = normalize(query_rows, totals_q, gain_q * (math.log2(math.e) / HEAD_DIM**0.5))
    key_norm = normalize(key_rows, totals_k, gain_k)
    live_rows = jnp.arange(capacity, dtype=jnp.int32) < my_length
    live = live_rows[None, :].astype(jnp.float32)
    own_label = (session[0] + 1).astype(jnp.bfloat16)
    edge_index = jnp.arange(EDGE, dtype=jnp.int32)
    blank = jnp.zeros((EDGE, width_here), jnp.bfloat16)

    def tail(rows):
        return lax.dynamic_slice_in_dim(jnp.concatenate([blank, rows], 0), my_length, EDGE, 0)

    def edge(keys, values, is_live):
        labels = jnp.where(is_live, own_label, jnp.bfloat16(0))
        return jnp.concatenate([keys, values, jnp.pad(labels[None, :], ((0, 15), (0, width_here - EDGE)))], 0)

    tails = edge(tail(key_norm), tail(value_rows), edge_index >= EDGE - my_length)
    fronts = edge(key_norm[:EDGE], value_rows[:EDGE], edge_index < my_length)
    from_left = passed_along(tails, "tile", 1)

    def spread(is_visible):
        bias = jnp.where(is_visible, 0.0, jnp.float32(HIDDEN))
        return jnp.broadcast_to(bias[:, None], (bias.shape[0], 128))

    def arrived(edge):
        return edge[2 * EDGE, :EDGE] == own_label, edge[:EDGE], edge[EDGE : 2 * EDGE]

    up, down = ring_pairs(count, 1), ring_pairs(count, -1)

    def moved(piece, pairs):
        return lax.ppermute(piece, "tile", pairs)

    def after(pieces, results):
        *pieces, top = lax.optimization_barrier((*pieces, results[0]))
        return pieces, [top, *results[1:]]

    keys, values = [mem_keys], [mem_values]
    for step in range(1, half):
        for pieces in (keys, values):
            pieces += [moved(pieces[-2 if step > 1 else -1], down), moved(pieces[-1], up)]
        if step == 1:
            from_left, *_ = lax.optimization_barrier((from_left, *values[1:]))
            seen, left_keys, left_values = arrived(from_left)
            bias = spread(jnp.concatenate([live_rows, seen]))
            sums = near_part(bias, query_norm, key_norm, value_rows, left_keys, left_values)
    keys.append(moved(keys[-1], up))
    values.append(moved(values[-2], down))

    most = 2 * request.shape[0] // count
    segments, starts = [], []
    for stage, (first, stop) in enumerate(stages(half)):
        size = stop - first
        (*pieces,), sums = after([*keys[first:stop], *values[first:stop]], sums)
        theirs = their_first[2 * first + size : 2 * stop + 1]
        limit = min(request.shape[0], size * most)
        picked = pick_part(f"pick_{stage}", theirs, their_block, limit, pieces[:size], pieces[size:])
        received = moved(picked, swap)
        if stage == 1:
            fronts, received = lax.optimization_barrier((fronts, received))
            seen, right_keys, right_values = arrived(passed_along(fronts, "tile", -1))
        segments.append([*pieces, received])
        starts.append(my_first[2 * first : 2 * first + size + 1])
        if stage > 0:
            bounds = jnp.concatenate([*starts, my_first[2 * stop :][:1]])
            slots = min(request.shape[0], sum(len(segment) // 2 for segment in segments) * 2 * most)
            final = live if first == 2 * half - 1 else None
            beside = (spread(seen), right_keys, right_values) if stage == 2 else ()
            sums = far_part(f"far_{stage}", bounds, my_block, slots, query_norm, sums, segments, final, beside)
            segments, starts = [], []
    return sums


def solution(mesh):
    in_specs = (
        P("tile", "head"),
        P("tile", "head"),
        P("tile", "head"),
        P("head"),
        P("head"),
        P("tile", None, "head"),
        P("tile", None, "head"),
        P("tile"),
        P("tile"),
        P("tile", None),
        P("tile"),
    )
    out_specs = P("tile", "head")
    return jax.shard_map(
        per_device, mesh=mesh, in_specs=in_specs, out_specs=out_specs, check_vma=False
    )
```

```python
import functools
import math

import jax
import jax.numpy as jnp
from jax import lax
from jax.experimental import pallas as pl
from jax.experimental.pallas import tpu as pltpu
from jax.sharding import PartitionSpec as P

HEAD_DIM = 128
WIDTH = 5120
EDGE = 64
EPSILON = 1e-06
HIDDEN = -1e30
VMEM_BYTES = 24 * 1024 * 1024


def passed_along(value, axis, steps):
    count = lax.axis_size(axis)
    first, last = (max(0, -steps), min(count, count - steps))
    return lax.ppermute(value, axis, [(source, source + steps) for source in range(first, last)])


def row_squares(raw_rows):
    rows32 = raw_rows.astype(jnp.float32)
    return jnp.sum(rows32 * rows32, axis=1)


def normalize(raw_rows, totals, gain):
    rows32 = raw_rows.astype(jnp.float32)
    factor = lax.rsqrt(totals / WIDTH + EPSILON)
    return (rows32 * factor[:, None] * gain).astype(jnp.bfloat16)


def chip_position(tile, levels):
    level, row = tile // 4, (tile // 2) % 2
    return level + row * (2 * levels - 1 - 2 * level)


def ring_pairs(count, step):
    levels = count // 4
    at = {(chip_position(t, levels), t % 2): t for t in range(count)}
    places = 2 * levels
    return [(at[p, c], at[(p + step) % places, c]) for p in range(places) for c in range(2)]


def across_t(first, second):
    return lax.dot_general(first, second, (((1,), (1,)), ((), ())), preferred_element_type=jnp.float32)


def down_rows(first, second):
    return lax.dot_general(first, second, (((0,), (0,)), ((), ())), preferred_element_type=jnp.float32)


def attend(heads):
    scores = []
    for query, parts, _ in heads:
        wide = [jnp.concatenate([bias] * (query.shape[0] // bias.shape[1]), axis=1) for _, _, bias in parts]
        scores.append([across_t(keys, query) + add for (keys, _, _), add in zip(parts, wide)])
    tops = []
    for group, (_, _, before) in zip(scores, heads):
        found = [jnp.max(part, axis=0, keepdims=True) for part in group]
        tops.append(functools.reduce(jnp.maximum, found if before is None else found + [before[0]]))
    weights = [[jnp.exp2(part - top) for part in group] for group, top in zip(scores, tops)]
    results = []
    for group, top, (_, parts, before) in zip(weights, tops, heads):
        total = sum(jnp.sum(part, axis=0, keepdims=True) for part in group)
        acc = sum(down_rows(values, part.astype(jnp.bfloat16)) for part, (_, values, _) in zip(group, parts))
        if before is not None:
            kept = jnp.exp2(before[0] - top)
            total = total + kept * before[1]
            acc = acc + kept * before[2]
        results.append((top, total, acc))
    return results


def store_sums(sums, head, place, top_ref, sum_ref, acc_ref):
    top, total, acc = sums
    top_ref[head] = jnp.broadcast_to(top, top_ref.shape[1:])
    sum_ref[head] = jnp.broadcast_to(total, sum_ref.shape[1:])
    acc_ref[place, :] = acc


def over_heads(width, body):
    heads = width // HEAD_DIM
    together = max(n for n in (1, 2, 4, 5) if heads % n == 0 and (n < 5 or heads < 10))

    def some(i, carry):
        numbers = [i * together + j for j in range(together)]
        body([(head, pl.ds(pl.multiple_of(head * HEAD_DIM, HEAD_DIM), HEAD_DIM)) for head in numbers])
        return carry

    lax.fori_loop(0, heads // together, some, 0)


def near_kernel(bias_ref, q_ref, k_ref, v_ref, ek_ref, ev_ref, top_ref, sum_ref, acc_ref):
    own = k_ref.shape[0]

    def body(places):
        heads = []
        for _, place in places:
            parts = [
                (k_ref[:, place], v_ref[:, place], bias_ref[:own, :]),
                (ek_ref[:, place], ev_ref[:, place], bias_ref[own:, :]),
            ]
            heads.append((q_ref[:, place], parts, None))
        for (head, place), sums in zip(places, attend(heads)):
            store_sums(sums, head, place, top_ref, sum_ref, acc_ref)

    over_heads(q_ref.shape[1], body)


def sum_shapes(rows, width):
    stat = jax.ShapeDtypeStruct((width // HEAD_DIM, 8, rows), jnp.float32)
    return [stat, stat, jax.ShapeDtypeStruct((width, rows), jnp.float32)]


IN_VMEM = pl.BlockSpec(memory_space=pltpu.VMEM)
IN_HBM = pl.BlockSpec(memory_space=pltpu.HBM)


def cost(rows, seen, width):
    return pl.CostEstimate(
        flops=4 * rows * seen * width,
        bytes_accessed=10 * rows * width,
        transcendentals=rows * seen * width // HEAD_DIM,
    )


def near_part(bias, query, keys, values, edge_keys, edge_values):
    rows, width = query.shape
    return pl.pallas_call(
        near_kernel,
        in_specs=[IN_VMEM] * 6,
        out_specs=[IN_VMEM] * 3,
        out_shape=sum_shapes(rows, width),
        compiler_params=pltpu.CompilerParams(vmem_limit_bytes=VMEM_BYTES),
        cost_estimate=cost(rows, bias.shape[0], width),
        name="near_part",
    )(bias, query, keys, values, edge_keys, edge_values)


def pick_kernel(groups, slots, first_ref, block_ref, *refs):
    key_pieces, value_pieces = refs[:groups], refs[groups : 2 * groups]
    picked, sem = refs[2 * groups :]
    start = first_ref[0]

    def fetch_from(g):
        def fetch(slot, carry):
            block = block_ref[slot]
            to = slot - start
            pltpu.make_async_copy(key_pieces[g].at[block], picked.at[to], sem).start()
            pltpu.make_async_copy(value_pieces[g].at[block], picked.at[slots + to], sem).start()
            return carry

        return fetch

    for g in range(groups):
        lax.fori_loop(first_ref[g], first_ref[g + 1], fetch_from(g), 0)
    lax.fori_loop(first_ref[groups], start + slots, fetch_from(0), 0)
    pltpu.make_async_copy(picked, picked, sem).wait()


def pick_part(name, first, block, slots, key_pieces, value_pieces):
    groups, (_, tokens, width) = len(key_pieces), key_pieces[0].shape
    block = jnp.concatenate([block, jnp.zeros((slots,), jnp.int32)])
    return pl.pallas_call(
        functools.partial(pick_kernel, groups, slots),
        in_specs=[pl.BlockSpec(memory_space=pltpu.SMEM)] * 2 + [IN_HBM] * (2 * groups),
        out_specs=IN_VMEM,
        out_shape=jax.ShapeDtypeStruct((2 * slots, tokens, width), jnp.bfloat16),
        scratch_shapes=[pltpu.SemaphoreType.DMA],
        compiler_params=pltpu.CompilerParams(vmem_limit_bytes=VMEM_BYTES),
        cost_estimate=pl.CostEstimate(flops=0, bytes_accessed=8 * slots * tokens * width, transcendentals=0),
        name=name,
    )(first, block, *key_pieces, *value_pieces)


def far_kernel(segments, last, beside, *refs):
    first_ref, block_ref, bias_ref, q_ref, before_top, before_sum, before_acc = refs[:7]
    refs = refs[7:]
    if last:
        live_ref, refs = refs[0], refs[1:]
    if beside:
        (beside_bias, beside_keys, beside_values), refs = refs[:3], refs[3:]
    *out_refs, keys, values, sems = refs[sum(2 * size + 1 for size in segments) :]
    slots, tokens = keys.shape[:2]
    start = first_ref[0]

    def fetch_one(key_block, value_block, to):
        pltpu.make_async_copy(key_block, keys.at[to], sems.at[0]).start()
        pltpu.make_async_copy(value_block, values.at[to], sems.at[1]).start()

    def fetch_from(key_piece, value_piece):
        def fetch(slot, carry):
            block = block_ref[slot]
            fetch_one(key_piece.at[block], value_piece.at[block], slot - start)
            return carry

        return fetch

    def fetch_received(received, base):
        def fetch(slot, carry):
            block = slot - base
            fetch_one(received.at[block], received.at[received.shape[0] // 2 + block], slot - start)
            return carry

        return fetch

    at, pieces = 0, refs
    for size in segments:
        for g in range(size):
            lax.fori_loop(first_ref[at], first_ref[at + 1], fetch_from(pieces[g], pieces[size + g]), 0)
            at += 1
        lax.fori_loop(first_ref[at], first_ref[at + 1], fetch_received(pieces[2 * size], first_ref[at]), 0)
        at += 1
        pieces = pieces[2 * size + 1 :]
    lax.fori_loop(first_ref[at], start + slots, fetch_from(refs[0], refs[segments[0]]), 0)
    pltpu.make_async_copy(keys, keys, sems.at[0]).wait()
    pltpu.make_async_copy(values, values, sems.at[1]).wait()

    def flat(array, place):
        block = array[:, :, place].astype(jnp.float32)
        return block.reshape(slots * tokens, HEAD_DIM).astype(jnp.bfloat16)

    def body(places):
        heads = []
        for head, place in places:
            before = (before_top[head][:1, :], before_sum[head][:1, :], before_acc[place, :])
            parts = [(flat(keys, place), flat(values, place), bias_ref[...])]
            if beside:
                parts.append((beside_keys[:, place], beside_values[:, place], beside_bias[...]))
            heads.append((q_ref[:, place], parts, before))
        for (head, place), sums in zip(places, attend(heads)):
            if last:
                result = jnp.where(live_ref[...] > 0.0, sums[2] / sums[1], 0.0)
                out_refs[0][:, place] = result.astype(out_refs[0].dtype).T
            else:
                store_sums(sums, head, place, *out_refs)

    over_heads(q_ref.shape[1], body)


def far_part(name, first, block, slots, query, before, segments, live=None, beside=()):
    rows, width = query.shape
    pieces = [array for segment in segments for array in segment]
    tokens = pieces[0].shape[1]
    seen = slots * tokens
    token = jnp.arange(seen, dtype=jnp.int32)[:, None]
    bias = jnp.where(token < (first[-1] - first[0]) * tokens, 0.0, jnp.float32(HIDDEN))
    bias = jnp.broadcast_to(bias, (seen, 128))
    block = jnp.concatenate([block, jnp.zeros((slots,), jnp.int32)])
    extra = ([] if live is None else [live]) + list(beside)
    final = jax.ShapeDtypeStruct((rows, width), jnp.bfloat16)
    return pl.pallas_call(
        functools.partial(far_kernel, [len(segment) // 2 for segment in segments], live is not None, len(beside) > 0),
        in_specs=[pl.BlockSpec(memory_space=pltpu.SMEM)] * 2
        + [IN_VMEM] * (5 + len(extra))
        + [IN_HBM] * len(pieces),
        out_specs=[IN_VMEM] * 3 if live is None else IN_VMEM,
        out_shape=sum_shapes(rows, width) if live is None else final,
        input_output_aliases={4: 0, 5: 1, 6: 2} if live is None else {},
        scratch_shapes=[
            pltpu.VMEM((slots, tokens, width), jnp.bfloat16),
            pltpu.VMEM((slots, tokens, width), jnp.bfloat16),
            pltpu.SemaphoreType.DMA((2,)),
        ],
        compiler_params=pltpu.CompilerParams(vmem_limit_bytes=VMEM_BYTES),
        cost_estimate=cost(rows, seen, width),
        name=name,
    )(first, block, bias, query, *before, *extra, *pieces)


def in_order(request, lane, owner_blocks, count, me):
    levels = count // 4
    places = 2 * levels
    half = places // 2
    owners, index = request // owner_blocks, request % owner_blocks
    ahead = (chip_position(owners, levels) - chip_position(me, levels)) % places
    distance = jnp.minimum(ahead, places - ahead)
    piece = jnp.where(distance == 0, 0, 2 * distance - 1 + (ahead > half).astype(jnp.int32))
    other = ((owners % 2) != lane).astype(jnp.int32)
    low, size = jnp.zeros_like(piece), jnp.zeros_like(piece)
    for first, stop in stages(half):
        inside = (piece >= first) & (piece < stop)
        low, size = jnp.where(inside, first, low), jnp.where(inside, stop - first, size)
    group = low + other * size + piece
    number = jnp.arange(group.shape[0], dtype=jnp.int32)
    rank_key = group * group.shape[0] + number
    rank = jnp.sum((rank_key[None, :] < rank_key[:, None]).astype(jnp.int32), axis=1)
    block = jnp.sum(jnp.where(rank[None, :] == number[:, None], index[None, :], 0), axis=1)
    groups = jnp.arange(2 * places + 1, dtype=jnp.int32)
    first = jnp.sum((group[None, :] < groups[:, None]).astype(jnp.int32), axis=1)
    return block, first


def stages(half):
    return (0, 2 * half - 5), (2 * half - 5, 2 * half - 3), (2 * half - 3, 2 * half - 1), (2 * half - 1, 2 * half)


def per_device(
    query_rows,
    key_rows,
    value_rows,
    gain_q,
    gain_k,
    mem_keys,
    mem_values,
    tile_len,
    session,
    req_owner,
    requested_block_index,
):
    capacity, width_here = query_rows.shape
    count = lax.axis_size("tile")
    levels = count // 4
    places = 2 * levels
    half = places // 2
    me = lax.axis_index("tile")

    swap = [(t, t ^ 1) for t in range(count)]
    owner_blocks = mem_keys.shape[0]
    request = req_owner[:, 0] * owner_blocks + requested_block_index
    my_block, my_first = in_order(request, me % 2, owner_blocks, count, me)
    plan = lax.ppermute(jnp.concatenate([my_first, my_block]), "tile", swap)
    their_first, their_block = plan[: my_first.shape[0]], plan[my_first.shape[0] :]

    my_length = tile_len[0]
    totals_q, totals_k = lax.psum((row_squares(query_rows), row_squares(key_rows)), "head")
    query_norm = normalize(query_rows, totals_q, gain_q * (math.log2(math.e) / HEAD_DIM**0.5))
    key_norm = normalize(key_rows, totals_k, gain_k)
    live_rows = jnp.arange(capacity, dtype=jnp.int32) < my_length
    live = live_rows[None, :].astype(jnp.float32)
    own_label = (session[0] + 1).astype(jnp.bfloat16)
    edge_index = jnp.arange(EDGE, dtype=jnp.int32)
    blank = jnp.zeros((EDGE, width_here), jnp.bfloat16)

    def tail(rows):
        return lax.dynamic_slice_in_dim(jnp.concatenate([blank, rows], 0), my_length, EDGE, 0)

    def edge(keys, values, is_live):
        labels = jnp.where(is_live, own_label, jnp.bfloat16(0))
        return jnp.concatenate([keys, values, jnp.pad(labels[None, :], ((0, 15), (0, width_here - EDGE)))], 0)

    tails = edge(tail(key_norm), tail(value_rows), edge_index >= EDGE - my_length)
    fronts = edge(key_norm[:EDGE], value_rows[:EDGE], edge_index < my_length)
    from_left = passed_along(tails, "tile", 1)

    def spread(is_visible):
        bias = jnp.where(is_visible, 0.0, jnp.float32(HIDDEN))
        return jnp.broadcast_to(bias[:, None], (bias.shape[0], 128))

    def arrived(edge):
        return edge[2 * EDGE, :EDGE] == own_label, edge[:EDGE], edge[EDGE : 2 * EDGE]

    up, down = ring_pairs(count, 1), ring_pairs(count, -1)

    def moved(piece, pairs):
        return lax.ppermute(piece, "tile", pairs)

    def after(pieces, results):
        *pieces, top = lax.optimization_barrier((*pieces, results[0]))
        return pieces, [top, *results[1:]]

    keys, values = [mem_keys], [mem_values]
    for step in range(1, half):
        for pieces in (keys, values):
            pieces += [moved(pieces[-2 if step > 1 else -1], down), moved(pieces[-1], up)]
        if step == 1:
            from_left, *_ = lax.optimization_barrier((from_left, *values[1:]))
            seen, left_keys, left_values = arrived(from_left)
            bias = spread(jnp.concatenate([live_rows, seen]))
            sums = near_part(bias, query_norm, key_norm, value_rows, left_keys, left_values)
    keys.append(moved(keys[-1], up))
    values.append(moved(values[-2], down))

    most = 2 * request.shape[0] // count
    segments, starts = [], []
    for stage, (first, stop) in enumerate(stages(half)):
        size = stop - first
        (*pieces,), sums = after([*keys[first:stop], *values[first:stop]], sums)
        if stage < 2:
            *pieces, values[stop], values[stop + 1] = lax.optimization_barrier(
                (*pieces, values[stop], values[stop + 1])
            )
        if stage == 2:
            *pieces, segments[0][-1] = lax.optimization_barrier((*pieces, segments[0][-1]))
        theirs = their_first[2 * first + size : 2 * stop + 1]
        limit = min(request.shape[0], size * most)
        picked = pick_part(f"pick_{stage}", theirs, their_block, limit, pieces[:size], pieces[size:])
        received = moved(picked, swap)
        if stage == 0:
            fronts, received = lax.optimization_barrier((fronts, received))
            seen, right_keys, right_values = arrived(passed_along(fronts, "tile", -1))
        segments.append([*pieces, received])
        starts.append(my_first[2 * first : 2 * first + size + 1])
        if stage != 1:
            bounds = jnp.concatenate([*starts, my_first[2 * stop :][:1]])
            slots = min(request.shape[0], sum(len(segment) // 2 for segment in segments) * 2 * most)
            final = live if first == 2 * half - 1 else None
            beside = (spread(seen), right_keys, right_values) if stage == 2 else ()
            sums = far_part(f"far_{stage}", bounds, my_block, slots, query_norm, sums, segments, final, beside)
            segments, starts = [], []
    return sums


def solution(mesh):
    in_specs = (
        P("tile", "head"),
        P("tile", "head"),
        P("tile", "head"),
        P("head"),
        P("head"),
        P("tile", None, "head"),
        P("tile", None, "head"),
        P("tile"),
        P("tile"),
        P("tile", None),
        P("tile"),
    )
    out_specs = P("tile", "head")
    return jax.shard_map(
        per_device, mesh=mesh, in_specs=in_specs, out_specs=out_specs, check_vma=False
    )
```

```python
import functools
import math

import jax
import jax.numpy as jnp
from jax import lax
from jax.experimental import pallas as pl
from jax.experimental.pallas import tpu as pltpu
from jax.sharding import PartitionSpec as P

HEAD_DIM = 128
WIDTH = 5120
EDGE = 64
EPSILON = 1e-06
HIDDEN = -1e30
VMEM_BYTES = 24 * 1024 * 1024


def passed_along(value, axis, steps):
    count = lax.axis_size(axis)
    first, last = (max(0, -steps), min(count, count - steps))
    return lax.ppermute(value, axis, [(source, source + steps) for source in range(first, last)])


def row_squares(raw_rows):
    rows32 = raw_rows.astype(jnp.float32)
    return jnp.sum(rows32 * rows32, axis=1)


def normalize(raw_rows, totals, gain):
    rows32 = raw_rows.astype(jnp.float32)
    factor = lax.rsqrt(totals / WIDTH + EPSILON)
    return (rows32 * factor[:, None] * gain).astype(jnp.bfloat16)


def chip_position(tile, levels):
    level, row = tile // 4, (tile // 2) % 2
    return level + row * (2 * levels - 1 - 2 * level)


def ring_pairs(count, step):
    levels = count // 4
    at = {(chip_position(t, levels), t % 2): t for t in range(count)}
    places = 2 * levels
    return [(at[p, c], at[(p + step) % places, c]) for p in range(places) for c in range(2)]


def across_t(first, second):
    return lax.dot_general(first, second, (((1,), (1,)), ((), ())), preferred_element_type=jnp.float32)


def down_rows(first, second):
    return lax.dot_general(first, second, (((0,), (0,)), ((), ())), preferred_element_type=jnp.float32)


def attend(heads):
    scores = []
    for query, parts, _ in heads:
        wide = [jnp.concatenate([bias] * (query.shape[0] // bias.shape[1]), axis=1) for _, _, bias in parts]
        scores.append([across_t(keys, query) + add for (keys, _, _), add in zip(parts, wide)])
    tops = []
    for group, (_, _, before) in zip(scores, heads):
        found = [jnp.max(part, axis=0, keepdims=True) for part in group]
        tops.append(functools.reduce(jnp.maximum, found if before is None else found + [before[0]]))
    weights = [[jnp.exp2(part - top) for part in group] for group, top in zip(scores, tops)]
    results = []
    for group, top, (_, parts, before) in zip(weights, tops, heads):
        total = sum(jnp.sum(part, axis=0, keepdims=True) for part in group)
        acc = sum(down_rows(values, part.astype(jnp.bfloat16)) for part, (_, values, _) in zip(group, parts))
        if before is not None:
            kept = jnp.exp2(before[0] - top)
            total = total + kept * before[1]
            acc = acc + kept * before[2]
        results.append((top, total, acc))
    return results


def store_sums(sums, head, place, top_ref, sum_ref, acc_ref):
    top, total, acc = sums
    top_ref[head] = jnp.broadcast_to(top, top_ref.shape[1:])
    sum_ref[head] = jnp.broadcast_to(total, sum_ref.shape[1:])
    acc_ref[place, :] = acc


def over_heads(width, body):
    heads = width // HEAD_DIM
    together = max(n for n in (1, 2, 4, 5) if heads % n == 0 and (n < 5 or heads < 10))

    def some(i, carry):
        numbers = [i * together + j for j in range(together)]
        body([(head, pl.ds(pl.multiple_of(head * HEAD_DIM, HEAD_DIM), HEAD_DIM)) for head in numbers])
        return carry

    lax.fori_loop(0, heads // together, some, 0)


def near_kernel(bias_ref, q_ref, k_ref, v_ref, ek_ref, ev_ref, top_ref, sum_ref, acc_ref):
    own = k_ref.shape[0]

    def body(places):
        heads = []
        for _, place in places:
            parts = [
                (k_ref[:, place], v_ref[:, place], bias_ref[:own, :]),
                (ek_ref[:, place], ev_ref[:, place], bias_ref[own:, :]),
            ]
            heads.append((q_ref[:, place], parts, None))
        for (head, place), sums in zip(places, attend(heads)):
            store_sums(sums, head, place, top_ref, sum_ref, acc_ref)

    over_heads(q_ref.shape[1], body)


def sum_shapes(rows, width):
    stat = jax.ShapeDtypeStruct((width // HEAD_DIM, 8, rows), jnp.float32)
    return [stat, stat, jax.ShapeDtypeStruct((width, rows), jnp.float32)]


IN_VMEM = pl.BlockSpec(memory_space=pltpu.VMEM)
IN_HBM = pl.BlockSpec(memory_space=pltpu.HBM)


def cost(rows, seen, width):
    return pl.CostEstimate(
        flops=4 * rows * seen * width,
        bytes_accessed=10 * rows * width,
        transcendentals=rows * seen * width // HEAD_DIM,
    )


def near_part(bias, query, keys, values, edge_keys, edge_values):
    rows, width = query.shape
    return pl.pallas_call(
        near_kernel,
        in_specs=[IN_VMEM] * 6,
        out_specs=[IN_VMEM] * 3,
        out_shape=sum_shapes(rows, width),
        compiler_params=pltpu.CompilerParams(vmem_limit_bytes=VMEM_BYTES),
        cost_estimate=cost(rows, bias.shape[0], width),
        name="near_part",
    )(bias, query, keys, values, edge_keys, edge_values)


def pick_kernel(groups, slots, first_ref, block_ref, *refs):
    key_pieces, value_pieces = refs[:groups], refs[groups : 2 * groups]
    picked_keys, picked_values, sems = refs[2 * groups :]
    start = first_ref[0]

    def fetch_from(g):
        def fetch(slot, carry):
            block = block_ref[slot]
            to = slot - start
            pltpu.make_async_copy(key_pieces[g].at[block], picked_keys.at[to], sems.at[0]).start()
            pltpu.make_async_copy(value_pieces[g].at[block], picked_values.at[to], sems.at[1]).start()
            return carry

        return fetch

    for g in range(groups):
        lax.fori_loop(first_ref[g], first_ref[g + 1], fetch_from(g), 0)
    lax.fori_loop(first_ref[groups], start + slots, fetch_from(0), 0)
    pltpu.make_async_copy(picked_keys, picked_keys, sems.at[0]).wait()
    pltpu.make_async_copy(picked_values, picked_values, sems.at[1]).wait()


def pick_part(name, first, block, slots, key_pieces, value_pieces):
    groups, (_, tokens, width) = len(key_pieces), key_pieces[0].shape
    block = jnp.concatenate([block, jnp.zeros((slots,), jnp.int32)])
    return pl.pallas_call(
        functools.partial(pick_kernel, groups, slots),
        in_specs=[pl.BlockSpec(memory_space=pltpu.SMEM)] * 2 + [IN_HBM] * (2 * groups),
        out_specs=[IN_VMEM] * 2,
        out_shape=[jax.ShapeDtypeStruct((slots, tokens, width), jnp.bfloat16)] * 2,
        scratch_shapes=[pltpu.SemaphoreType.DMA((2,))],
        compiler_params=pltpu.CompilerParams(vmem_limit_bytes=VMEM_BYTES),
        cost_estimate=pl.CostEstimate(flops=0, bytes_accessed=8 * slots * tokens * width, transcendentals=0),
        name=name,
    )(first, block, *key_pieces, *value_pieces)


def far_kernel(segments, last, beside, *refs):
    first_ref, block_ref, bias_ref, q_ref, before_top, before_sum, before_acc = refs[:7]
    refs = refs[7:]
    if last:
        live_ref, refs = refs[0], refs[1:]
    if beside:
        (beside_bias, beside_keys, beside_values), refs = refs[:3], refs[3:]
    *out_refs, keys, values, sems = refs[sum(2 * (size + got) for size, got in segments) :]
    slots, tokens = keys.shape[:2]
    start = first_ref[0]

    def fetch_one(key_block, value_block, to):
        pltpu.make_async_copy(key_block, keys.at[to], sems.at[0]).start()
        pltpu.make_async_copy(value_block, values.at[to], sems.at[1]).start()

    def fetch_from(key_piece, value_piece):
        def fetch(slot, carry):
            block = block_ref[slot]
            fetch_one(key_piece.at[block], value_piece.at[block], slot - start)
            return carry

        return fetch

    def fetch_received(received_keys, received_values, base):
        def fetch(slot, carry):
            fetch_one(received_keys.at[slot - base], received_values.at[slot - base], slot - start)
            return carry

        return fetch

    at, pieces, spare = 0, refs, None
    for size, got in segments:
        for g in range(size):
            spare = (pieces[g], pieces[size + g])
            lax.fori_loop(first_ref[at], first_ref[at + 1], fetch_from(*spare), 0)
            at += 1
        pieces = pieces[2 * size :]
        if got:
            lax.fori_loop(first_ref[at], first_ref[at + 1], fetch_received(pieces[0], pieces[1], first_ref[at]), 0)
            at, pieces = at + 1, pieces[2:]
    lax.fori_loop(first_ref[at], start + slots, fetch_from(*spare), 0)
    pltpu.make_async_copy(keys, keys, sems.at[0]).wait()
    pltpu.make_async_copy(values, values, sems.at[1]).wait()

    def flat(array, place):
        block = array[:, :, place].astype(jnp.float32)
        return block.reshape(slots * tokens, HEAD_DIM).astype(jnp.bfloat16)

    def body(places):
        heads = []
        for head, place in places:
            before = (before_top[head][:1, :], before_sum[head][:1, :], before_acc[place, :])
            parts = [(flat(keys, place), flat(values, place), bias_ref[...])]
            if beside:
                parts.append((beside_keys[:, place], beside_values[:, place], beside_bias[...]))
            heads.append((q_ref[:, place], parts, before))
        for (head, place), sums in zip(places, attend(heads)):
            if last:
                result = jnp.where(live_ref[...] > 0.0, sums[2] / sums[1], 0.0)
                out_refs[0][:, place] = result.astype(out_refs[0].dtype).T
            else:
                store_sums(sums, head, place, *out_refs)

    over_heads(q_ref.shape[1], body)


def far_part(name, first, block, slots, query, before, segments, live=None, beside=()):
    rows, width = query.shape
    pieces = [array for own, received in segments for array in (*own, *received)]
    sizes = [(len(own) // 2, len(received) // 2) for own, received in segments]
    tokens = pieces[0].shape[1]
    seen = slots * tokens
    token = jnp.arange(seen, dtype=jnp.int32)[:, None]
    bias = jnp.where(token < (first[-1] - first[0]) * tokens, 0.0, jnp.float32(HIDDEN))
    bias = jnp.broadcast_to(bias, (seen, 128))
    block = jnp.concatenate([block, jnp.zeros((slots,), jnp.int32)])
    extra = ([] if live is None else [live]) + list(beside)
    final = jax.ShapeDtypeStruct((rows, width), jnp.bfloat16)
    return pl.pallas_call(
        functools.partial(far_kernel, sizes, live is not None, len(beside) > 0),
        in_specs=[pl.BlockSpec(memory_space=pltpu.SMEM)] * 2
        + [IN_VMEM] * (5 + len(extra))
        + [IN_HBM] * len(pieces),
        out_specs=[IN_VMEM] * 3 if live is None else IN_VMEM,
        out_shape=sum_shapes(rows, width) if live is None else final,
        input_output_aliases={4: 0, 5: 1, 6: 2} if live is None else {},
        scratch_shapes=[
            pltpu.VMEM((slots, tokens, width), jnp.bfloat16),
            pltpu.VMEM((slots, tokens, width), jnp.bfloat16),
            pltpu.SemaphoreType.DMA((2,)),
        ],
        compiler_params=pltpu.CompilerParams(vmem_limit_bytes=VMEM_BYTES),
        cost_estimate=cost(rows, seen, width),
        name=name,
    )(first, block, bias, query, *before, *extra, *pieces)


def in_order(request, lane, owner_blocks, count, me):
    levels = count // 4
    places = 2 * levels
    half = places // 2
    owners, index = request // owner_blocks, request % owner_blocks
    ahead = (chip_position(owners, levels) - chip_position(me, levels)) % places
    distance = jnp.minimum(ahead, places - ahead)
    piece = jnp.where(distance == 0, 0, 2 * distance - 1 + (ahead > half).astype(jnp.int32))
    other = ((owners % 2) != lane).astype(jnp.int32)
    low, size = jnp.zeros_like(piece), jnp.zeros_like(piece)
    for first, stop in stages(half):
        inside = (piece >= first) & (piece < stop)
        low, size = jnp.where(inside, first, low), jnp.where(inside, stop - first, size)
    group = low + other * size + piece
    number = jnp.arange(group.shape[0], dtype=jnp.int32)
    rank_key = group * group.shape[0] + number
    rank = jnp.sum((rank_key[None, :] < rank_key[:, None]).astype(jnp.int32), axis=1)
    block = jnp.sum(jnp.where(rank[None, :] == number[:, None], index[None, :], 0), axis=1)
    groups = jnp.arange(2 * places + 1, dtype=jnp.int32)
    first = jnp.sum((group[None, :] < groups[:, None]).astype(jnp.int32), axis=1)
    return block, first


def stages(half):
    return (0, 2 * half - 5), (2 * half - 5, 2 * half - 3), (2 * half - 3, 2 * half - 1), (2 * half - 1, 2 * half)


def per_device(
    query_rows,
    key_rows,
    value_rows,
    gain_q,
    gain_k,
    mem_keys,
    mem_values,
    tile_len,
    session,
    req_owner,
    requested_block_index,
):
    capacity, width_here = query_rows.shape
    count = lax.axis_size("tile")
    levels = count // 4
    places = 2 * levels
    half = places // 2
    me = lax.axis_index("tile")

    swap = [(t, t ^ 1) for t in range(count)]
    owner_blocks = mem_keys.shape[0]
    request = req_owner[:, 0] * owner_blocks + requested_block_index
    my_block, my_first = in_order(request, me % 2, owner_blocks, count, me)
    plan = lax.ppermute(jnp.concatenate([my_first, my_block]), "tile", swap)
    their_first, their_block = plan[: my_first.shape[0]], plan[my_first.shape[0] :]

    my_length = tile_len[0]
    totals_q, totals_k = lax.psum((row_squares(query_rows), row_squares(key_rows)), "head")
    query_norm = normalize(query_rows, totals_q, gain_q * (math.log2(math.e) / HEAD_DIM**0.5))
    key_norm = normalize(key_rows, totals_k, gain_k)
    live_rows = jnp.arange(capacity, dtype=jnp.int32) < my_length
    live = live_rows[None, :].astype(jnp.float32)
    own_label = (session[0] + 1).astype(jnp.bfloat16)
    edge_index = jnp.arange(EDGE, dtype=jnp.int32)
    blank = jnp.zeros((EDGE, width_here), jnp.bfloat16)

    def tail(rows):
        return lax.dynamic_slice_in_dim(jnp.concatenate([blank, rows], 0), my_length, EDGE, 0)

    def edge(keys, values, is_live):
        labels = jnp.where(is_live, own_label, jnp.bfloat16(0))
        return jnp.concatenate([keys, values, jnp.pad(labels[None, :], ((0, 15), (0, width_here - EDGE)))], 0)

    tails = edge(tail(key_norm), tail(value_rows), edge_index >= EDGE - my_length)
    fronts = edge(key_norm[:EDGE], value_rows[:EDGE], edge_index < my_length)
    from_left = passed_along(tails, "tile", 1)

    def spread(is_visible):
        bias = jnp.where(is_visible, 0.0, jnp.float32(HIDDEN))
        return jnp.broadcast_to(bias[:, None], (bias.shape[0], 128))

    def arrived(edge):
        return edge[2 * EDGE, :EDGE] == own_label, edge[:EDGE], edge[EDGE : 2 * EDGE]

    up, down = ring_pairs(count, 1), ring_pairs(count, -1)

    def moved(piece, pairs):
        return lax.ppermute(piece, "tile", pairs)

    def after(pieces, results):
        *pieces, top = lax.optimization_barrier((*pieces, results[0]))
        return pieces, [top, *results[1:]]

    keys, values = [mem_keys], [mem_values]
    for step in range(1, half):
        for pieces in (keys, values):
            pieces += [moved(pieces[-2 if step > 1 else -1], down), moved(pieces[-1], up)]
        if step == 1:
            from_left, *_ = lax.optimization_barrier((from_left, *values[1:]))
            seen, left_keys, left_values = arrived(from_left)
            bias = spread(jnp.concatenate([live_rows, seen]))
            sums = near_part(bias, query_norm, key_norm, value_rows, left_keys, left_values)
    keys.append(moved(keys[-1], up))
    values.append(moved(values[-2], down))

    most = 2 * request.shape[0] // count
    segments, starts, slots = [], [], 0
    for stage, (first, stop) in enumerate(stages(half)):
        size = stop - first
        limit = min(request.shape[0], size * most)
        (*pieces,), sums = after([*keys[first:stop], *values[first:stop]], sums)
        middle, end = 2 * first + size, 2 * stop
        if stage == 1:
            segments.append((pieces, ()))
            bounds = jnp.concatenate([*starts, my_first[2 * first : middle + 1]])
            slots = min(request.shape[0], slots + limit)
            sums = far_part("far_1", bounds, my_block, slots, query_norm, sums, segments)
            (*pieces,), sums = after(pieces, sums)
            segments, starts, slots = [], [], 0
        if stage == 2:
            *pieces, late = lax.optimization_barrier((*pieces, segments[0][1][0]))
            segments[0] = ((), [late, segments[0][1][1]])
        theirs = their_first[middle : end + 1]
        picked = pick_part(f"pick_{stage}", theirs, their_block, limit, pieces[:size], pieces[size:])
        received = [moved(array, swap) for array in picked]
        if stage == 0:
            fronts, received[0] = lax.optimization_barrier((fronts, received[0]))
            seen, right_keys, right_values = arrived(passed_along(fronts, "tile", -1))
        segments.append((() if stage == 1 else pieces, received))
        starts.append(my_first[middle if stage == 1 else 2 * first : middle + 1])
        slots += limit if stage == 1 else 2 * limit
        if stage > 1:
            bounds = jnp.concatenate([*starts, my_first[end:][:1]])
            slots = min(request.shape[0], slots)
            final = live if stage == 3 else None
            beside = (spread(seen), right_keys, right_values) if stage == 2 else ()
            sums = far_part(f"far_{stage}", bounds, my_block, slots, query_norm, sums, segments, final, beside)
            segments, starts, slots = [], [], 0
    return sums


def solution(mesh):
    in_specs = (
        P("tile", "head"),
        P("tile", "head"),
        P("tile", "head"),
        P("head"),
        P("head"),
        P("tile", None, "head"),
        P("tile", None, "head"),
        P("tile"),
        P("tile"),
        P("tile", None),
        P("tile"),
    )
    out_specs = P("tile", "head")
    return jax.shard_map(
        per_device, mesh=mesh, in_specs=in_specs, out_specs=out_specs, check_vma=False
    )
```

```python
import functools
import math

import jax
import jax.numpy as jnp
from jax import lax
from jax.experimental import pallas as pl
from jax.experimental.pallas import tpu as pltpu
from jax.sharding import PartitionSpec as P

HEAD_DIM = 128
WIDTH = 5120
EDGE = 64
EPSILON = 1e-06
HIDDEN = -1e30
VMEM_BYTES = 24 * 1024 * 1024


def passed_along(value, axis, steps):
    count = lax.axis_size(axis)
    first, last = (max(0, -steps), min(count, count - steps))
    return lax.ppermute(value, axis, [(source, source + steps) for source in range(first, last)])


def row_squares(raw_rows):
    rows32 = raw_rows.astype(jnp.float32)
    return jnp.sum(rows32 * rows32, axis=1)


def normalize(raw_rows, totals, gain):
    rows32 = raw_rows.astype(jnp.float32)
    factor = lax.rsqrt(totals / WIDTH + EPSILON)
    return (rows32 * factor[:, None] * gain).astype(jnp.bfloat16)


def chip_position(tile, levels):
    level, row = tile // 4, (tile // 2) % 2
    return level + row * (2 * levels - 1 - 2 * level)


def ring_pairs(count, step):
    levels = count // 4
    at = {(chip_position(t, levels), t % 2): t for t in range(count)}
    places = 2 * levels
    return [(at[p, c], at[(p + step) % places, c]) for p in range(places) for c in range(2)]


def across_t(first, second):
    return lax.dot_general(first, second, (((1,), (1,)), ((), ())), preferred_element_type=jnp.float32)


def down_rows(first, second):
    return lax.dot_general(first, second, (((0,), (0,)), ((), ())), preferred_element_type=jnp.float32)


def attend(heads):
    scores = []
    for query, parts, _ in heads:
        wide = [jnp.concatenate([bias] * (query.shape[0] // bias.shape[1]), axis=1) for _, _, bias in parts]
        scores.append([across_t(keys, query) + add for (keys, _, _), add in zip(parts, wide)])
    tops = []
    for group, (_, _, before) in zip(scores, heads):
        found = [jnp.max(part, axis=0, keepdims=True) for part in group]
        tops.append(functools.reduce(jnp.maximum, found if before is None else found + [before[0]]))
    weights = [[jnp.exp2(part - top) for part in group] for group, top in zip(scores, tops)]
    results = []
    for group, top, (_, parts, before) in zip(weights, tops, heads):
        total = sum(jnp.sum(part, axis=0, keepdims=True) for part in group)
        acc = sum(down_rows(values, part.astype(jnp.bfloat16)) for part, (_, values, _) in zip(group, parts))
        if before is not None:
            kept = jnp.exp2(before[0] - top)
            total = total + kept * before[1]
            acc = acc + kept * before[2]
        results.append((top, total, acc))
    return results


def store_sums(sums, head, place, top_ref, sum_ref, acc_ref):
    top, total, acc = sums
    top_ref[head] = jnp.broadcast_to(top, top_ref.shape[1:])
    sum_ref[head] = jnp.broadcast_to(total, sum_ref.shape[1:])
    acc_ref[place, :] = acc


def over_heads(width, body):
    heads = width // HEAD_DIM
    together = max(n for n in (1, 2, 4, 5) if heads % n == 0 and (n < 5 or heads < 10))

    def some(i, carry):
        numbers = [i * together + j for j in range(together)]
        body([(head, pl.ds(pl.multiple_of(head * HEAD_DIM, HEAD_DIM), HEAD_DIM)) for head in numbers])
        return carry

    lax.fori_loop(0, heads // together, some, 0)


def near_kernel(bias_ref, q_ref, k_ref, v_ref, ek_ref, ev_ref, top_ref, sum_ref, acc_ref):
    own = k_ref.shape[0]

    def body(places):
        heads = []
        for _, place in places:
            parts = [
                (k_ref[:, place], v_ref[:, place], bias_ref[:own, :]),
                (ek_ref[:, place], ev_ref[:, place], bias_ref[own:, :]),
            ]
            heads.append((q_ref[:, place], parts, None))
        for (head, place), sums in zip(places, attend(heads)):
            store_sums(sums, head, place, top_ref, sum_ref, acc_ref)

    over_heads(q_ref.shape[1], body)


def sum_shapes(rows, width):
    stat = jax.ShapeDtypeStruct((width // HEAD_DIM, 8, rows), jnp.float32)
    return [stat, stat, jax.ShapeDtypeStruct((width, rows), jnp.float32)]


IN_VMEM = pl.BlockSpec(memory_space=pltpu.VMEM)
IN_HBM = pl.BlockSpec(memory_space=pltpu.HBM)


def cost(rows, seen, width):
    return pl.CostEstimate(
        flops=4 * rows * seen * width,
        bytes_accessed=10 * rows * width,
        transcendentals=rows * seen * width // HEAD_DIM,
    )


def near_part(bias, query, keys, values, edge_keys, edge_values):
    rows, width = query.shape
    return pl.pallas_call(
        near_kernel,
        in_specs=[IN_VMEM] * 6,
        out_specs=[IN_VMEM] * 3,
        out_shape=sum_shapes(rows, width),
        compiler_params=pltpu.CompilerParams(vmem_limit_bytes=VMEM_BYTES),
        cost_estimate=cost(rows, bias.shape[0], width),
        name="near_part",
    )(bias, query, keys, values, edge_keys, edge_values)


def pick_kernel(groups, slots, first_ref, block_ref, *refs):
    key_pieces, value_pieces = refs[:groups], refs[groups : 2 * groups]
    picked_keys, picked_values, sems = refs[2 * groups :]
    start = first_ref[0]

    def fetch_from(g):
        def fetch(slot, carry):
            block = block_ref[slot]
            to = slot - start
            pltpu.make_async_copy(key_pieces[g].at[block], picked_keys.at[to], sems.at[0]).start()
            pltpu.make_async_copy(value_pieces[g].at[block], picked_values.at[to], sems.at[1]).start()
            return carry

        return fetch

    for g in range(groups):
        lax.fori_loop(first_ref[g], first_ref[g + 1], fetch_from(g), 0)
    lax.fori_loop(first_ref[groups], start + slots, fetch_from(0), 0)
    pltpu.make_async_copy(picked_keys, picked_keys, sems.at[0]).wait()
    pltpu.make_async_copy(picked_values, picked_values, sems.at[1]).wait()


def pick_part(name, first, block, slots, key_pieces, value_pieces):
    groups, (_, tokens, width) = len(key_pieces), key_pieces[0].shape
    block = jnp.concatenate([block, jnp.zeros((slots,), jnp.int32)])
    return pl.pallas_call(
        functools.partial(pick_kernel, groups, slots),
        in_specs=[pl.BlockSpec(memory_space=pltpu.SMEM)] * 2 + [IN_HBM] * (2 * groups),
        out_specs=[IN_VMEM] * 2,
        out_shape=[jax.ShapeDtypeStruct((slots, tokens, width), jnp.bfloat16)] * 2,
        scratch_shapes=[pltpu.SemaphoreType.DMA((2,))],
        compiler_params=pltpu.CompilerParams(vmem_limit_bytes=VMEM_BYTES),
        cost_estimate=pl.CostEstimate(flops=0, bytes_accessed=8 * slots * tokens * width, transcendentals=0),
        name=name,
    )(first, block, *key_pieces, *value_pieces)


def far_kernel(segments, last, beside, *refs):
    first_ref, block_ref, bias_ref, q_ref, before_top, before_sum, before_acc = refs[:7]
    refs = refs[7:]
    if last:
        live_ref, refs = refs[0], refs[1:]
    if beside:
        (beside_bias, beside_keys, beside_values), refs = refs[:3], refs[3:]
    *out_refs, keys, values, sems = refs[sum(2 * (size + got) for size, got in segments) :]
    slots, tokens = keys.shape[:2]
    start = first_ref[0]

    def fetch_one(key_block, value_block, to):
        pltpu.make_async_copy(key_block, keys.at[to], sems.at[0]).start()
        pltpu.make_async_copy(value_block, values.at[to], sems.at[1]).start()

    def fetch_from(key_piece, value_piece):
        def fetch(slot, carry):
            block = block_ref[slot]
            fetch_one(key_piece.at[block], value_piece.at[block], slot - start)
            return carry

        return fetch

    def fetch_received(received_keys, received_values, base):
        def fetch(slot, carry):
            fetch_one(received_keys.at[slot - base], received_values.at[slot - base], slot - start)
            return carry

        return fetch

    at, pieces, spare = 0, refs, None
    for size, got in segments:
        for g in range(size):
            spare = (pieces[g], pieces[size + g])
            lax.fori_loop(first_ref[at], first_ref[at + 1], fetch_from(*spare), 0)
            at += 1
        pieces = pieces[2 * size :]
        if got:
            lax.fori_loop(first_ref[at], first_ref[at + 1], fetch_received(pieces[0], pieces[1], first_ref[at]), 0)
            at, pieces = at + 1, pieces[2:]
    lax.fori_loop(first_ref[at], start + slots, fetch_from(*spare), 0)
    pltpu.make_async_copy(keys, keys, sems.at[0]).wait()
    pltpu.make_async_copy(values, values, sems.at[1]).wait()

    def flat(array, place):
        block = array[:, :, place].astype(jnp.float32)
        return block.reshape(slots * tokens, HEAD_DIM).astype(jnp.bfloat16)

    def body(places):
        heads = []
        for head, place in places:
            before = (before_top[head][:1, :], before_sum[head][:1, :], before_acc[place, :])
            parts = [(flat(keys, place), flat(values, place), bias_ref[...])]
            if beside:
                parts.append((beside_keys[:, place], beside_values[:, place], beside_bias[...]))
            heads.append((q_ref[:, place], parts, before))
        for (head, place), sums in zip(places, attend(heads)):
            if last:
                result = jnp.where(live_ref[...] > 0.0, sums[2] / sums[1], 0.0)
                out_refs[0][:, place] = result.astype(out_refs[0].dtype).T
            else:
                store_sums(sums, head, place, *out_refs)

    over_heads(q_ref.shape[1], body)


def far_part(name, first, block, slots, query, before, segments, live=None, beside=()):
    rows, width = query.shape
    pieces = [array for own, received in segments for array in (*own, *received)]
    sizes = [(len(own) // 2, len(received) // 2) for own, received in segments]
    tokens = pieces[0].shape[1]
    seen = slots * tokens
    token = jnp.arange(seen, dtype=jnp.int32)[:, None]
    bias = jnp.where(token < (first[-1] - first[0]) * tokens, 0.0, jnp.float32(HIDDEN))
    bias = jnp.broadcast_to(bias, (seen, 128))
    block = jnp.concatenate([block, jnp.zeros((slots,), jnp.int32)])
    extra = ([] if live is None else [live]) + list(beside)
    final = jax.ShapeDtypeStruct((rows, width), jnp.bfloat16)
    return pl.pallas_call(
        functools.partial(far_kernel, sizes, live is not None, len(beside) > 0),
        in_specs=[pl.BlockSpec(memory_space=pltpu.SMEM)] * 2
        + [IN_VMEM] * (5 + len(extra))
        + [IN_HBM] * len(pieces),
        out_specs=[IN_VMEM] * 3 if live is None else IN_VMEM,
        out_shape=sum_shapes(rows, width) if live is None else final,
        input_output_aliases={4: 0, 5: 1, 6: 2} if live is None else {},
        scratch_shapes=[
            pltpu.VMEM((slots, tokens, width), jnp.bfloat16),
            pltpu.VMEM((slots, tokens, width), jnp.bfloat16),
            pltpu.SemaphoreType.DMA((2,)),
        ],
        compiler_params=pltpu.CompilerParams(vmem_limit_bytes=VMEM_BYTES),
        cost_estimate=cost(rows, seen, width),
        name=name,
    )(first, block, bias, query, *before, *extra, *pieces)


def in_order(request, lane, owner_blocks, count, me):
    levels = count // 4
    places = 2 * levels
    half = places // 2
    owners, index = request // owner_blocks, request % owner_blocks
    ahead = (chip_position(owners, levels) - chip_position(me, levels)) % places
    distance = jnp.minimum(ahead, places - ahead)
    piece = jnp.where(distance == 0, 0, 2 * distance - 1 + (ahead > half).astype(jnp.int32))
    other = ((owners % 2) != lane).astype(jnp.int32)
    low, size = jnp.zeros_like(piece), jnp.zeros_like(piece)
    for first, stop in stages(half):
        inside = (piece >= first) & (piece < stop)
        low, size = jnp.where(inside, first, low), jnp.where(inside, stop - first, size)
    group = low + other * size + piece
    number = jnp.arange(group.shape[0], dtype=jnp.int32)
    rank_key = group * group.shape[0] + number
    rank = jnp.sum((rank_key[None, :] < rank_key[:, None]).astype(jnp.int32), axis=1)
    block = jnp.sum(jnp.where(rank[None, :] == number[:, None], index[None, :], 0), axis=1)
    groups = jnp.arange(2 * places + 1, dtype=jnp.int32)
    first = jnp.sum((group[None, :] < groups[:, None]).astype(jnp.int32), axis=1)
    return block, first


def stages(half):
    return (0, 2 * half - 5), (2 * half - 5, 2 * half - 3), (2 * half - 3, 2 * half - 1), (2 * half - 1, 2 * half)


def per_device(
    query_rows,
    key_rows,
    value_rows,
    gain_q,
    gain_k,
    mem_keys,
    mem_values,
    tile_len,
    session,
    req_owner,
    requested_block_index,
):
    capacity, width_here = query_rows.shape
    count = lax.axis_size("tile")
    levels = count // 4
    places = 2 * levels
    half = places // 2
    me = lax.axis_index("tile")

    swap = [(t, t ^ 1) for t in range(count)]
    owner_blocks = mem_keys.shape[0]
    request = req_owner[:, 0] * owner_blocks + requested_block_index
    my_block, my_first = in_order(request, me % 2, owner_blocks, count, me)
    plan = lax.ppermute(jnp.concatenate([my_first, my_block]), "tile", swap)
    their_first, their_block = plan[: my_first.shape[0]], plan[my_first.shape[0] :]

    my_length = tile_len[0]
    totals_q, totals_k = lax.psum((row_squares(query_rows), row_squares(key_rows)), "head")
    query_norm = normalize(query_rows, totals_q, gain_q * (math.log2(math.e) / HEAD_DIM**0.5))
    key_norm = normalize(key_rows, totals_k, gain_k)
    live_rows = jnp.arange(capacity, dtype=jnp.int32) < my_length
    live = live_rows[None, :].astype(jnp.float32)
    own_label = (session[0] + 1).astype(jnp.bfloat16)
    edge_index = jnp.arange(EDGE, dtype=jnp.int32)
    blank = jnp.zeros((EDGE, width_here), jnp.bfloat16)

    def tail(rows):
        return lax.dynamic_slice_in_dim(jnp.concatenate([blank, rows], 0), my_length, EDGE, 0)

    def edge(keys, values, is_live):
        labels = jnp.where(is_live, own_label, jnp.bfloat16(0))
        return jnp.concatenate([keys, values, jnp.pad(labels[None, :], ((0, 15), (0, width_here - EDGE)))], 0)

    tails = edge(tail(key_norm), tail(value_rows), edge_index >= EDGE - my_length)
    fronts = edge(key_norm[:EDGE], value_rows[:EDGE], edge_index < my_length)
    from_left = passed_along(tails, "tile", 1)

    def spread(is_visible):
        bias = jnp.where(is_visible, 0.0, jnp.float32(HIDDEN))
        return jnp.broadcast_to(bias[:, None], (bias.shape[0], 128))

    def arrived(edge):
        return edge[2 * EDGE, :EDGE] == own_label, edge[:EDGE], edge[EDGE : 2 * EDGE]

    up, down = ring_pairs(count, 1), ring_pairs(count, -1)

    def moved(piece, pairs):
        return lax.ppermute(piece, "tile", pairs)

    def after(pieces, results):
        *pieces, top = lax.optimization_barrier((*pieces, results[0]))
        return pieces, [top, *results[1:]]

    keys, values = [mem_keys], [mem_values]
    for step in range(1, half):
        for pieces in (keys, values):
            pieces += [moved(pieces[-2 if step > 1 else -1], down), moved(pieces[-1], up)]
        if step == 1:
            from_left, *_ = lax.optimization_barrier((from_left, *keys[1:], *values[1:]))
            seen, left_keys, left_values = arrived(from_left)
            bias = spread(jnp.concatenate([live_rows, seen]))
            sums = near_part(bias, query_norm, key_norm, value_rows, left_keys, left_values)
    keys.append(moved(keys[-1], up))
    values.append(moved(values[-2], down))

    most = 2 * request.shape[0] // count
    segments, starts, slots = [], [], 0
    for stage, (first, stop) in enumerate(stages(half)):
        size = stop - first
        limit = min(request.shape[0], size * most)
        (*pieces,), sums = after([*keys[first:stop], *values[first:stop]], sums)
        middle, end = 2 * first + size, 2 * stop
        if stage == 1:
            segments.append((pieces, ()))
            bounds = jnp.concatenate([*starts, my_first[2 * first : middle + 1]])
            slots = min(request.shape[0], slots + limit)
            sums = far_part("far_1", bounds, my_block, slots, query_norm, sums, segments)
            (*pieces,), sums = after(pieces, sums)
            segments, starts, slots = [], [], 0
        if stage == 2:
            *pieces, late = lax.optimization_barrier((*pieces, segments[0][1][0]))
            segments[0] = ((), [late, segments[0][1][1]])
        theirs = their_first[middle : end + 1]
        picked = pick_part(f"pick_{stage}", theirs, their_block, limit, pieces[:size], pieces[size:])
        received = [moved(array, swap) for array in picked]
        if stage == 0:
            fronts, received[0] = lax.optimization_barrier((fronts, received[0]))
            seen, right_keys, right_values = arrived(passed_along(fronts, "tile", -1))
        segments.append((() if stage == 1 else pieces, received))
        starts.append(my_first[middle if stage == 1 else 2 * first : middle + 1])
        slots += limit if stage == 1 else 2 * limit
        if stage > 1:
            bounds = jnp.concatenate([*starts, my_first[end:][:1]])
            slots = min(request.shape[0], slots)
            final = live if stage == 3 else None
            beside = (spread(seen), right_keys, right_values) if stage == 2 else ()
            sums = far_part(f"far_{stage}", bounds, my_block, slots, query_norm, sums, segments, final, beside)
            segments, starts, slots = [], [], 0
    return sums


def solution(mesh):
    in_specs = (
        P("tile", "head"),
        P("tile", "head"),
        P("tile", "head"),
        P("head"),
        P("head"),
        P("tile", None, "head"),
        P("tile", None, "head"),
        P("tile"),
        P("tile"),
        P("tile", None),
        P("tile"),
    )
    out_specs = P("tile", "head")
    return jax.shard_map(
        per_device, mesh=mesh, in_specs=in_specs, out_specs=out_specs, check_vma=False
    )
```

```python
import functools
import math

import jax
import jax.numpy as jnp
from jax import lax
from jax.experimental import pallas as pl
from jax.experimental.pallas import tpu as pltpu
from jax.sharding import PartitionSpec as P

HEAD_DIM = 128
WIDTH = 5120
EDGE = 64
EPSILON = 1e-06
HIDDEN = -1e30
VMEM_BYTES = 24 * 1024 * 1024


def passed_along(value, axis, steps):
    count = lax.axis_size(axis)
    first, last = (max(0, -steps), min(count, count - steps))
    return lax.ppermute(value, axis, [(source, source + steps) for source in range(first, last)])


def row_squares(raw_rows):
    rows32 = raw_rows.astype(jnp.float32)
    return jnp.sum(rows32 * rows32, axis=1)


def normalize(raw_rows, totals, gain):
    rows32 = raw_rows.astype(jnp.float32)
    factor = lax.rsqrt(totals / WIDTH + EPSILON)
    return (rows32 * factor[:, None] * gain).astype(jnp.bfloat16)


def chip_position(tile, levels):
    level, row = tile // 4, (tile // 2) % 2
    return level + row * (2 * levels - 1 - 2 * level)


def ring_pairs(count, step):
    levels = count // 4
    at = {(chip_position(t, levels), t % 2): t for t in range(count)}
    places = 2 * levels
    return [(at[p, c], at[(p + step) % places, c]) for p in range(places) for c in range(2)]


def across_t(first, second):
    return lax.dot_general(first, second, (((1,), (1,)), ((), ())), preferred_element_type=jnp.float32)


def down_rows(first, second):
    return lax.dot_general(first, second, (((0,), (0,)), ((), ())), preferred_element_type=jnp.float32)


def attend(heads):
    scores = []
    for query, parts, _ in heads:
        wide = [jnp.concatenate([bias] * (query.shape[0] // bias.shape[1]), axis=1) for _, _, bias in parts]
        scores.append([across_t(keys, query) + add for (keys, _, _), add in zip(parts, wide)])
    tops = []
    for group, (_, _, before) in zip(scores, heads):
        found = [jnp.max(part, axis=0, keepdims=True) for part in group]
        tops.append(functools.reduce(jnp.maximum, found if before is None else found + [before[0]]))
    weights = [[jnp.exp2(part - top) for part in group] for group, top in zip(scores, tops)]
    results = []
    for group, top, (_, parts, before) in zip(weights, tops, heads):
        total = sum(jnp.sum(part, axis=0, keepdims=True) for part in group)
        acc = sum(down_rows(values, part.astype(jnp.bfloat16)) for part, (_, values, _) in zip(group, parts))
        if before is not None:
            kept = jnp.exp2(before[0] - top)
            total = total + kept * before[1]
            acc = acc + kept * before[2]
        results.append((top, total, acc))
    return results


def store_sums(sums, head, place, top_ref, sum_ref, acc_ref):
    top, total, acc = sums
    top_ref[head] = jnp.broadcast_to(top, top_ref.shape[1:])
    sum_ref[head] = jnp.broadcast_to(total, sum_ref.shape[1:])
    acc_ref[place, :] = acc


def over_heads(width, body):
    heads = width // HEAD_DIM
    together = max(n for n in (1, 2, 4, 5) if heads % n == 0 and (n < 5 or heads < 10))

    def some(i, carry):
        numbers = [i * together + j for j in range(together)]
        body([(head, pl.ds(pl.multiple_of(head * HEAD_DIM, HEAD_DIM), HEAD_DIM)) for head in numbers])
        return carry

    lax.fori_loop(0, heads // together, some, 0)


def near_kernel(bias_ref, q_ref, k_ref, v_ref, ek_ref, ev_ref, top_ref, sum_ref, acc_ref):
    own = k_ref.shape[0]

    def body(places):
        heads = []
        for _, place in places:
            parts = [
                (k_ref[:, place], v_ref[:, place], bias_ref[:own, :]),
                (ek_ref[:, place], ev_ref[:, place], bias_ref[own:, :]),
            ]
            heads.append((q_ref[:, place], parts, None))
        for (head, place), sums in zip(places, attend(heads)):
            store_sums(sums, head, place, top_ref, sum_ref, acc_ref)

    over_heads(q_ref.shape[1], body)


def sum_shapes(rows, width):
    stat = jax.ShapeDtypeStruct((width // HEAD_DIM, 8, rows), jnp.float32)
    return [stat, stat, jax.ShapeDtypeStruct((width, rows), jnp.float32)]


IN_VMEM = pl.BlockSpec(memory_space=pltpu.VMEM)
IN_HBM = pl.BlockSpec(memory_space=pltpu.HBM)


def cost(rows, seen, width):
    return pl.CostEstimate(
        flops=4 * rows * seen * width,
        bytes_accessed=10 * rows * width,
        transcendentals=rows * seen * width // HEAD_DIM,
    )


def near_part(bias, query, keys, values, edge_keys, edge_values):
    rows, width = query.shape
    return pl.pallas_call(
        near_kernel,
        in_specs=[IN_VMEM] * 6,
        out_specs=[IN_VMEM] * 3,
        out_shape=sum_shapes(rows, width),
        compiler_params=pltpu.CompilerParams(vmem_limit_bytes=VMEM_BYTES),
        cost_estimate=cost(rows, bias.shape[0], width),
        name="near_part",
    )(bias, query, keys, values, edge_keys, edge_values)


def pick_kernel(groups, slots, first_ref, block_ref, *refs):
    key_pieces, value_pieces = refs[:groups], refs[groups : 2 * groups]
    picked_keys, picked_values, sems = refs[2 * groups :]
    start = first_ref[0]

    def fetch_from(g):
        def fetch(slot, carry):
            block = block_ref[slot]
            to = slot - start
            pltpu.make_async_copy(key_pieces[g].at[block], picked_keys.at[to], sems.at[0]).start()
            pltpu.make_async_copy(value_pieces[g].at[block], picked_values.at[to], sems.at[1]).start()
            return carry

        return fetch

    for g in range(groups):
        lax.fori_loop(first_ref[g], first_ref[g + 1], fetch_from(g), 0)
    lax.fori_loop(first_ref[groups], start + slots, fetch_from(0), 0)
    pltpu.make_async_copy(picked_keys, picked_keys, sems.at[0]).wait()
    pltpu.make_async_copy(picked_values, picked_values, sems.at[1]).wait()


def pick_part(name, first, block, slots, key_pieces, value_pieces):
    groups, (_, tokens, width) = len(key_pieces), key_pieces[0].shape
    block = jnp.concatenate([block, jnp.zeros((slots,), jnp.int32)])
    return pl.pallas_call(
        functools.partial(pick_kernel, groups, slots),
        in_specs=[pl.BlockSpec(memory_space=pltpu.SMEM)] * 2 + [IN_HBM] * (2 * groups),
        out_specs=[IN_VMEM] * 2,
        out_shape=[jax.ShapeDtypeStruct((slots, tokens, width), jnp.bfloat16)] * 2,
        scratch_shapes=[pltpu.SemaphoreType.DMA((2,))],
        compiler_params=pltpu.CompilerParams(vmem_limit_bytes=VMEM_BYTES),
        cost_estimate=pl.CostEstimate(flops=0, bytes_accessed=8 * slots * tokens * width, transcendentals=0),
        name=name,
    )(first, block, *key_pieces, *value_pieces)


def far_kernel(segments, last, beside, *refs):
    first_ref, block_ref, bias_ref, q_ref, before_top, before_sum, before_acc = refs[:7]
    refs = refs[7:]
    if last:
        live_ref, refs = refs[0], refs[1:]
    if beside:
        (beside_bias, beside_keys, beside_values), refs = refs[:3], refs[3:]
    *out_refs, keys, values, sems = refs[sum(2 * (size + got) for size, got in segments) :]
    slots, tokens = keys.shape[:2]
    start = first_ref[0]

    def fetch_one(key_block, value_block, to):
        pltpu.make_async_copy(key_block, keys.at[to], sems.at[0]).start()
        pltpu.make_async_copy(value_block, values.at[to], sems.at[1]).start()

    def fetch_from(key_piece, value_piece):
        def fetch(slot, carry):
            block = block_ref[slot]
            fetch_one(key_piece.at[block], value_piece.at[block], slot - start)
            return carry

        return fetch

    def fetch_received(received_keys, received_values, base):
        def fetch(slot, carry):
            fetch_one(received_keys.at[slot - base], received_values.at[slot - base], slot - start)
            return carry

        return fetch

    at, pieces, spare = 0, refs, None
    for size, got in segments:
        for g in range(size):
            spare = (pieces[g], pieces[size + g])
            lax.fori_loop(first_ref[at], first_ref[at + 1], fetch_from(*spare), 0)
            at += 1
        pieces = pieces[2 * size :]
        if got:
            lax.fori_loop(first_ref[at], first_ref[at + 1], fetch_received(pieces[0], pieces[1], first_ref[at]), 0)
            at, pieces = at + 1, pieces[2:]
    lax.fori_loop(first_ref[at], start + slots, fetch_from(*spare), 0)
    pltpu.make_async_copy(keys, keys, sems.at[0]).wait()
    pltpu.make_async_copy(values, values, sems.at[1]).wait()

    def flat(array, place):
        block = array[:, :, place].astype(jnp.float32)
        return block.reshape(slots * tokens, HEAD_DIM).astype(jnp.bfloat16)

    def body(places):
        heads = []
        for head, place in places:
            before = (before_top[head][:1, :], before_sum[head][:1, :], before_acc[place, :])
            parts = [(flat(keys, place), flat(values, place), bias_ref[...])]
            if beside:
                parts.append((beside_keys[:, place], beside_values[:, place], beside_bias[...]))
            heads.append((q_ref[:, place], parts, before))
        for (head, place), sums in zip(places, attend(heads)):
            if last:
                result = jnp.where(live_ref[...] > 0.0, sums[2] / sums[1], 0.0)
                out_refs[0][:, place] = result.astype(out_refs[0].dtype).T
            else:
                store_sums(sums, head, place, *out_refs)

    over_heads(q_ref.shape[1], body)


def far_part(name, first, block, slots, query, before, segments, live=None, beside=()):
    rows, width = query.shape
    pieces = [array for own, received in segments for array in (*own, *received)]
    sizes = [(len(own) // 2, len(received) // 2) for own, received in segments]
    tokens = pieces[0].shape[1]
    seen = slots * tokens
    token = jnp.arange(seen, dtype=jnp.int32)[:, None]
    bias = jnp.where(token < (first[-1] - first[0]) * tokens, 0.0, jnp.float32(HIDDEN))
    bias = jnp.broadcast_to(bias, (seen, 128))
    block = jnp.concatenate([block, jnp.zeros((slots,), jnp.int32)])
    extra = ([] if live is None else [live]) + list(beside)
    final = jax.ShapeDtypeStruct((rows, width), jnp.bfloat16)
    return pl.pallas_call(
        functools.partial(far_kernel, sizes, live is not None, len(beside) > 0),
        in_specs=[pl.BlockSpec(memory_space=pltpu.SMEM)] * 2
        + [IN_VMEM] * (5 + len(extra))
        + [IN_HBM] * len(pieces),
        out_specs=[IN_VMEM] * 3 if live is None else IN_VMEM,
        out_shape=sum_shapes(rows, width) if live is None else final,
        input_output_aliases={4: 0, 5: 1, 6: 2} if live is None else {},
        scratch_shapes=[
            pltpu.VMEM((slots, tokens, width), jnp.bfloat16),
            pltpu.VMEM((slots, tokens, width), jnp.bfloat16),
            pltpu.SemaphoreType.DMA((2,)),
        ],
        compiler_params=pltpu.CompilerParams(vmem_limit_bytes=VMEM_BYTES),
        cost_estimate=cost(rows, seen, width),
        name=name,
    )(first, block, bias, query, *before, *extra, *pieces)


def in_order(request, lane, owner_blocks, count, me):
    levels = count // 4
    places = 2 * levels
    half = places // 2
    owners, index = request // owner_blocks, request % owner_blocks
    ahead = (chip_position(owners, levels) - chip_position(me, levels)) % places
    distance = jnp.minimum(ahead, places - ahead)
    piece = jnp.where(distance == 0, 0, 2 * distance - 1 + (ahead > half).astype(jnp.int32))
    other = ((owners % 2) != lane).astype(jnp.int32)
    low, size = jnp.zeros_like(piece), jnp.zeros_like(piece)
    for first, stop in stages(half):
        inside = (piece >= first) & (piece < stop)
        low, size = jnp.where(inside, first, low), jnp.where(inside, stop - first, size)
    group = low + other * size + piece
    number = jnp.arange(group.shape[0], dtype=jnp.int32)
    rank_key = group * group.shape[0] + number
    rank = jnp.sum((rank_key[None, :] < rank_key[:, None]).astype(jnp.int32), axis=1)
    block = jnp.sum(jnp.where(rank[None, :] == number[:, None], index[None, :], 0), axis=1)
    groups = jnp.arange(2 * places + 1, dtype=jnp.int32)
    first = jnp.sum((group[None, :] < groups[:, None]).astype(jnp.int32), axis=1)
    return block, first


def stages(half):
    return (0, 2 * half - 5), (2 * half - 5, 2 * half - 3), (2 * half - 3, 2 * half - 1), (2 * half - 1, 2 * half)


def per_device(
    query_rows,
    key_rows,
    value_rows,
    gain_q,
    gain_k,
    mem_keys,
    mem_values,
    tile_len,
    session,
    req_owner,
    requested_block_index,
):
    capacity, width_here = query_rows.shape
    count = lax.axis_size("tile")
    levels = count // 4
    places = 2 * levels
    half = places // 2
    me = lax.axis_index("tile")

    swap = [(t, t ^ 1) for t in range(count)]
    owner_blocks = mem_keys.shape[0]
    request = req_owner[:, 0] * owner_blocks + requested_block_index
    my_block, my_first = in_order(request, me % 2, owner_blocks, count, me)
    plan = lax.ppermute(jnp.concatenate([my_first, my_block]), "tile", swap)
    their_first, their_block = plan[: my_first.shape[0]], plan[my_first.shape[0] :]

    my_length = tile_len[0]
    totals_q, totals_k = lax.psum((row_squares(query_rows), row_squares(key_rows)), "head")
    query_norm = normalize(query_rows, totals_q, gain_q * (math.log2(math.e) / HEAD_DIM**0.5))
    key_norm = normalize(key_rows, totals_k, gain_k)
    live_rows = jnp.arange(capacity, dtype=jnp.int32) < my_length
    live = live_rows[None, :].astype(jnp.float32)
    own_label = (session[0] + 1).astype(jnp.bfloat16)
    edge_index = jnp.arange(EDGE, dtype=jnp.int32)
    blank = jnp.zeros((EDGE, width_here), jnp.bfloat16)

    def tail(rows):
        return lax.dynamic_slice_in_dim(jnp.concatenate([blank, rows], 0), my_length, EDGE, 0)

    def edge(keys, values, is_live):
        labels = jnp.where(is_live, own_label, jnp.bfloat16(0))
        return jnp.concatenate([keys, values, jnp.pad(labels[None, :], ((0, 15), (0, width_here - EDGE)))], 0)

    tails = edge(tail(key_norm), tail(value_rows), edge_index >= EDGE - my_length)
    fronts = edge(key_norm[:EDGE], value_rows[:EDGE], edge_index < my_length)
    from_left = passed_along(tails, "tile", 1)

    def spread(is_visible):
        bias = jnp.where(is_visible, 0.0, jnp.float32(HIDDEN))
        return jnp.broadcast_to(bias[:, None], (bias.shape[0], 128))

    def arrived(edge):
        return edge[2 * EDGE, :EDGE] == own_label, edge[:EDGE], edge[EDGE : 2 * EDGE]

    up, down = ring_pairs(count, 1), ring_pairs(count, -1)

    def moved(piece, pairs):
        return lax.ppermute(piece, "tile", pairs)

    def after(pieces, results):
        *pieces, top = lax.optimization_barrier((*pieces, results[0]))
        return pieces, [top, *results[1:]]

    keys, values = [mem_keys], [mem_values]
    for step in range(1, half):
        for pieces in (keys, values):
            pieces += [moved(pieces[-2 if step > 1 else -1], down), moved(pieces[-1], up)]
        if step == 1:
            from_left, *_ = lax.optimization_barrier((from_left, *values[1:]))
            seen, left_keys, left_values = arrived(from_left)
            bias = spread(jnp.concatenate([live_rows, seen]))
            sums = near_part(bias, query_norm, key_norm, value_rows, left_keys, left_values)
    keys.append(moved(keys[-1], up))
    values.append(moved(values[-2], down))

    most = 2 * request.shape[0] // count
    segments, starts, slots = [], [], 0
    for stage, (first, stop) in enumerate(stages(half)):
        size = stop - first
        limit = min(request.shape[0], size * most)
        (*pieces,), sums = after([*keys[first:stop], *values[first:stop]], sums)
        middle, end = 2 * first + size, 2 * stop
        if stage == 1:
            segments.append((pieces, ()))
            bounds = jnp.concatenate([*starts, my_first[2 * first : middle + 1]])
            slots = min(request.shape[0], slots + limit)
            sums = far_part("far_1", bounds, my_block, slots, query_norm, sums, segments)
            (*pieces,), sums = after(pieces, sums)
            segments, starts, slots = [], [], 0
        if stage == 2:
            *pieces, late = lax.optimization_barrier((*pieces, segments[0][1][0]))
            segments[0] = ((), [late, segments[0][1][1]])
        if stage == 3:
            both = [array for piece in pieces for array in (piece, moved(piece, swap))]
            bounds = my_first[2 * first : end + 1]
            return far_part("far_3", bounds, my_block, 2 * limit, query_norm, sums, [(both, ())], live)
        theirs = their_first[middle : end + 1]
        picked = pick_part(f"pick_{stage}", theirs, their_block, limit, pieces[:size], pieces[size:])
        received = [moved(array, swap) for array in picked]
        if stage == 0:
            fronts, received[0] = lax.optimization_barrier((fronts, received[0]))
            seen, right_keys, right_values = arrived(passed_along(fronts, "tile", -1))
        segments.append((() if stage == 1 else pieces, received))
        starts.append(my_first[middle if stage == 1 else 2 * first : middle + 1])
        slots += limit if stage == 1 else 2 * limit
        if stage > 1:
            bounds = jnp.concatenate([*starts, my_first[end:][:1]])
            slots = min(request.shape[0], slots)
            beside = (spread(seen), right_keys, right_values)
            sums = far_part("far_2", bounds, my_block, slots, query_norm, sums, segments, None, beside)


def solution(mesh):
    in_specs = (
        P("tile", "head"),
        P("tile", "head"),
        P("tile", "head"),
        P("head"),
        P("head"),
        P("tile", None, "head"),
        P("tile", None, "head"),
        P("tile"),
        P("tile"),
        P("tile", None),
        P("tile"),
    )
    out_specs = P("tile", "head")
    return jax.shard_map(
        per_device, mesh=mesh, in_specs=in_specs, out_specs=out_specs, check_vma=False
    )
```
